512 devices in a mesh: st: 128 (over z, y, core), hd: 4 (over x).
Axes of the slice: x: 4, y: 8, z: 8, core: 2. Of those that a mesh axis runs over, the one named last changes fastest.
Arguments:
- event_queries: bfloat16 [65536, 1024], P('st', 'hd'), may hold values from -10 to 10
- event_values: bfloat16 [65536, 1024], P('st', 'hd'), may hold values from -64 to 64
- frame_keys: bfloat16 [65536, 1024], P('st', 'hd'), may hold values from -10 to 10
- frame_values: bfloat16 [65536, 1024], P('st', 'hd'), may hold values from -64 to 64
- partner: int32 [256, 3], P('st'), may hold values from 0 to 255, as said below
- live_count: int32 [256], P('st'), may hold values from 1 to 3
- event_cotangent: bfloat16 [65536, 1024], P('st', 'hd'), may hold values from -6 to 6
- frame_cotangent: bfloat16 [65536, 1024], P('st', 'hd'), may hold values from -6 to 6
Outputs:
- event_out: bfloat16 [65536, 1024], P('st', 'hd')
- frame_out: bfloat16 [65536, 1024], P('st', 'hd')
- grad_queries: bfloat16 [65536, 1024], P('st', 'hd')
- grad_event_values: bfloat16 [65536, 1024], P('st', 'hd')
- grad_keys: bfloat16 [65536, 1024], P('st', 'hd')
- grad_frame_values: bfloat16 [65536, 1024], P('st', 'hd')
The draws below stay inside these ranges and needn't reach their ends.
Inputs may be any that keep to these rules, and one draw needn't show every extreme that they name: `partner`: slot 0 of event block a is frame block a; the live slots of a name distinct frame blocks f with f // 2 between a // 2 - 1 and a // 2 + 1; the other slots hold a.
All inputs are finite; a program needn't handle non-finite values.
Results may differ from the reference program's by a relative error of at most 0.022.
Values may be sent and summed in bfloat16 or wider, within the bound.
No kernel may reach another device: no remote copies, remote signals or barrier semaphores. Data moves between devices by JAX's collectives and lax.ppermute only.
A program may use at most 64 MiB of HBM per device.

```python
import math
import jax
import jax.numpy as jnp
from jax import lax

HEADS = 16
DH = 64
BLOCK = 256
BLK_DEV = 2
SLOTS = 3
REACH = 1
EBLOCKS = 256
TOKENS = 65536
N_ST = 128


def slot_counts(key):
    counts = jax.random.randint(jax.random.fold_in(key, 7), (EBLOCKS,), 1, SLOTS + 1)
    busiest = jax.random.randint(jax.random.fold_in(key, 8), (), 0, EBLOCKS)
    quietest = (busiest + 1 + jax.random.randint(jax.random.fold_in(key, 9), (), 0, EBLOCKS - 1)) % EBLOCKS
    return counts.at[busiest].set(SLOTS).at[quietest].set(1)


def draw_live_count(key, part):
    return slot_counts(key).astype(jnp.int32)


def draw_partner(key, part):
    counts = slot_counts(key)
    key = jax.random.fold_in(key, 3)
    span = (2 * REACH + 1) * BLK_DEV
    own = jnp.arange(EBLOCKS, dtype=jnp.int32)
    starts = (own // BLK_DEV - REACH) * BLK_DEV
    offsets = jnp.arange(span, dtype=jnp.int32)
    nearby = starts[:, None] + offsets[None, :]
    usable = (nearby >= 0) & (nearby < EBLOCKS) & (nearby != own[:, None])
    ranks = jax.random.randint(key, (EBLOCKS, span), 0, 1 << 20) * span + offsets[None, :]
    ranks = jnp.where(usable, ranks, -1 - offsets[None, :])
    _, order = lax.top_k(ranks, SLOTS - 1)
    picked = jnp.take_along_axis(nearby, order, axis=1)
    table = jnp.concatenate([own[:, None], picked], axis=1)
    unused = jnp.arange(SLOTS)[None, :] >= counts[:, None]
    return jnp.where(unused, own[:, None], table).astype(jnp.int32)


def draw_event_queries(key, part):
    key = jax.random.fold_in(key, 31)
    return jax.random.truncated_normal(key, -6.0, 6.0, (TOKENS, HEADS * DH), jnp.float32).astype(jnp.bfloat16)


def draw_frame_keys(key, part):
    key = jax.random.fold_in(key, 32)
    return jax.random.truncated_normal(key, -6.0, 6.0, (TOKENS, HEADS * DH), jnp.float32).astype(jnp.bfloat16)


def value_scales(key):
    head = (jnp.arange(HEADS * DH) // DH).astype(jnp.float32)
    rising = 3.0 ** (head / (HEADS - 1))
    spread = jnp.exp(jax.random.uniform(jax.random.fold_in(key, 41), (HEADS * DH,), jnp.float32, 0.0, math.log(3.3)))
    row_scale = jnp.exp(jax.random.uniform(jax.random.fold_in(key, 42), (TOKENS, 1), jnp.float32, 0.0, math.log(10.0))) / 3.16
    return row_scale * (rising * spread / 3.0)[None, :]


def value_draw(key):
    scales = value_scales(key)
    return jax.random.truncated_normal(jax.random.fold_in(key, 45), -6.0, 6.0, (TOKENS, HEADS * DH), jnp.float32) * scales


def draw_event_values(key, part):
    key = jax.random.fold_in(key, 51)
    return value_draw(key).astype(jnp.bfloat16)


def draw_frame_values(key, part):
    key = jax.random.fold_in(key, 61)
    return value_draw(key).astype(jnp.bfloat16)


def levels(own_key, shape, pieces, least, top_value):
    def one(axis_at, blocks):
        heights = jax.random.uniform(jax.random.fold_in(jax.random.fold_in(own_key, 6), axis_at), (blocks,), jnp.float32, least / len(pieces), top_value / len(pieces))
        return jnp.repeat(jnp.exp(heights), shape[axis_at] // blocks).reshape((-1,) + (1,) * (len(shape) - axis_at - 1))

    level = one(*pieces[0])
    for cut in pieces[1:]:
        level = level * one(*cut)
    return level


def gaussian(key, extent, scale, bound, cuts=(), held_as=jnp.bfloat16):
    entries = jax.random.normal(key, extent, jnp.float32) * scale
    if len(cuts) > 0:
        entries = levels(key, extent, cuts, -0.22, 0.18) * entries
    return jnp.clip(entries, min=-bound, max=bound).astype(held_as)


def setup_inputs(seed: int = 0) -> dict:
    seeds = jax.random.split(jax.random.key(seed), 9)
    return {
        "event_queries": draw_event_queries(jax.random.fold_in(seeds[8], 71), 0),
        "event_values": draw_event_values(jax.random.fold_in(seeds[8], 71), 0),
        "frame_keys": draw_frame_keys(jax.random.fold_in(seeds[8], 71), 0),
        "frame_values": draw_frame_values(jax.random.fold_in(seeds[8], 71), 0),
        "partner": draw_partner(jax.random.fold_in(seeds[8], 71), 0),
        "live_count": draw_live_count(jax.random.fold_in(seeds[8], 71), 0),
        "event_cotangent": gaussian(seeds[6], (TOKENS, HEADS * DH), 1.0, 6.0, ((0, 128), (1, 4))),
        "frame_cotangent": gaussian(seeds[7], (TOKENS, HEADS * DH), 1.0, 6.0, ((0, 128), (1, 4))),
    }


NEG = -1e+30
EPS = 1e-06

def to_bfloat(values):
    return lax.optimization_barrier(values.astype(jnp.bfloat16)).astype(jnp.float32)

def row_probs(scores, live_slots):
    masked = jnp.where(live_slots[None, None, :, None], scores, NEG)
    top = lax.optimization_barrier(jnp.max(masked, axis=(2, 3), keepdims=True))
    expo = jnp.exp(masked - top)
    return expo / lax.optimization_barrier(jnp.sum(expo, axis=(2, 3), keepdims=True))

def reference(event_queries, event_values, frame_keys, frame_values, partner, live_count, event_cotangent, frame_cotangent):
    width = HEADS * DH
    scale = DH ** (-0.5)

    def blocks(values):
        return values.astype(jnp.float32).reshape(EBLOCKS, BLOCK, HEADS, DH)
    query_blocks = blocks(event_queries)
    event_blocks = blocks(event_values)
    key_blocks = blocks(frame_keys)
    frame_blocks = blocks(frame_values)
    live = jnp.arange(SLOTS)[None, :] < live_count[:, None]
    live_tiles = live[:, :, None, None]

    def scores_of(queries, slots):
        return scale * jnp.einsum('ihd,sjhd->hisj', queries, key_blocks[slots])

    def first_pass(item):
        queries, slots, live_slots = item
        scores = scores_of(queries, slots)
        weights = to_bfloat(row_probs(scores, live_slots))
        attended = jnp.einsum('hisj,sjhd->ihd', weights, frame_blocks[slots])
        top = lax.optimization_barrier(jnp.max(scores, axis=1))
        tile_sum = lax.optimization_barrier(jnp.sum(jnp.exp(scores - top[:, None]), axis=1))
        return (attended, jnp.transpose(top, (1, 0, 2)), jnp.transpose(tile_sum, (1, 0, 2)))
    event_att, tile_top, tile_sum = lax.map(first_pass, (query_blocks, partner, live))
    tile_top = jnp.where(live_tiles, tile_top, NEG)
    col_max = jnp.full((EBLOCKS, HEADS, BLOCK), NEG, jnp.float32).at[partner].max(tile_top)
    ratio = jnp.exp(tile_top - col_max[partner])
    col_total = jnp.zeros((EBLOCKS, HEADS, BLOCK), jnp.float32).at[partner].add(ratio * tile_sum)
    factor = ratio / col_total[partner]

    def second_pass(carry, item):
        queries, values, slots, tile_factor = item
        scores = scores_of(queries, slots)
        top = lax.optimization_barrier(jnp.max(scores, axis=1, keepdims=True))
        weights = to_bfloat(jnp.exp(scores - top))
        tile = jnp.einsum('hisj,ihd->sjhd', weights, values)
        tile = tile * jnp.transpose(tile_factor, (0, 2, 1))[:, :, :, None]
        return (carry.at[slots].add(tile), None)
    frame_att, _ = lax.scan(second_pass, jnp.zeros((EBLOCKS, BLOCK, HEADS, DH), jnp.float32), (query_blocks, event_blocks, partner, factor))
    event_flat = event_att.reshape(TOKENS, width)
    frame_flat = frame_att.reshape(TOKENS, width)
    event_rms = lax.rsqrt(lax.optimization_barrier(jnp.sum(event_flat * event_flat, axis=1, keepdims=True)) / width + EPS)
    frame_rms = lax.rsqrt(lax.optimization_barrier(jnp.sum(frame_flat * frame_flat, axis=1, keepdims=True)) / width + EPS)
    event_normed = event_flat * event_rms
    frame_normed = frame_flat * frame_rms
    event_out = event_normed.astype(jnp.bfloat16)
    frame_out = frame_normed.astype(jnp.bfloat16)
    event_cot = event_cotangent.astype(jnp.float32)
    frame_cot = frame_cotangent.astype(jnp.float32)
    event_slope = lax.optimization_barrier(jnp.sum(event_cot * event_normed, axis=1, keepdims=True)) / width
    frame_slope = lax.optimization_barrier(jnp.sum(frame_cot * frame_normed, axis=1, keepdims=True)) / width
    event_grad = (event_rms * (event_cot - event_normed * event_slope)).astype(jnp.bfloat16)
    frame_grad = (frame_rms * (frame_cot - frame_normed * frame_slope)).astype(jnp.bfloat16)
    event_grad_blocks = blocks(event_grad)
    frame_grad_blocks = blocks(frame_grad)
    event_delta = lax.optimization_barrier(jnp.sum(event_grad_blocks * event_att, axis=3))
    frame_delta = jnp.transpose(lax.optimization_barrier(jnp.sum(frame_grad_blocks * frame_att, axis=3)), (0, 2, 1))

    def backward_block(item):
        queries, values, grads, delta, slots, live_slots = item
        keys = key_blocks[slots]
        frame_vals = frame_blocks[slots]
        frame_grads = frame_grad_blocks[slots]
        scores = scale * jnp.einsum('ihd,sjhd->hisj', queries, keys)
        row_p = row_probs(scores, live_slots)
        col_top = jnp.transpose(col_max[slots], (1, 0, 2))[:, None]
        col_sum = jnp.transpose(col_total[slots], (1, 0, 2))[:, None]
        col_delta = jnp.transpose(frame_delta[slots], (1, 0, 2))[:, None]
        col_p = jnp.where(live_slots[None, None, :, None], jnp.exp(scores - col_top) / col_sum, 0.0)
        row_change = jnp.einsum('ihd,sjhd->hisj', grads, frame_vals)
        col_change = jnp.einsum('ihd,sjhd->hisj', values, frame_grads)
        slope = to_bfloat(scale * (row_p * (row_change - jnp.transpose(delta)[:, :, None, None]) + col_p * (col_change - col_delta)))
        grad_q = jnp.einsum('hisj,sjhd->ihd', slope, keys).astype(jnp.bfloat16)
        grad_v = jnp.einsum('hisj,sjhd->ihd', to_bfloat(col_p), frame_grads).astype(jnp.bfloat16)
        key_part = jnp.einsum('hisj,ihd->sjhd', slope, queries)
        value_part = jnp.einsum('hisj,ihd->sjhd', to_bfloat(row_p), grads)
        return (grad_q, grad_v, key_part, value_part)
    span = 3 * BLK_DEV
    window_ids = jnp.arange(span, dtype=jnp.int32)
    centre = ((window_ids >= BLK_DEV) & (window_ids < 2 * BLK_DEV))[:, None, None, None]

    def backward_run(carry, item):
        key_sum, value_sum = carry
        run, queries, values, grads, delta, slots, live_slots = item
        grad_q, grad_v, key_part, value_part = lax.map(backward_block, (queries, values, grads, delta, slots, live_slots))
        window_slot = slots - (run - 1) * BLK_DEV
        select = ((window_slot[:, :, None] == window_ids[None, None, :]) & live_slots[:, :, None]).astype(jnp.float32)
        start = (run * BLK_DEV).astype(jnp.int32)
        zero = jnp.zeros((), jnp.int32)

        def collect(parts, total):
            window = jnp.einsum('tsw,tsjhd->wjhd', select, parts, precision=lax.Precision.HIGHEST)
            window = jnp.where(centre, window, to_bfloat(window))
            old = lax.dynamic_slice(total, (start, zero, zero, zero), (span, BLOCK, HEADS, DH))
            return lax.dynamic_update_slice(total, old + window, (start, zero, zero, zero))
        return ((collect(key_part, key_sum), collect(value_part, value_sum)), (grad_q, grad_v))

    def by_run(values):
        return values.reshape((N_ST, BLK_DEV) + values.shape[1:])
    zeros = jnp.zeros((EBLOCKS + 2 * BLK_DEV, BLOCK, HEADS, DH), jnp.float32)
    (key_sum, value_sum), (grad_q, grad_v) = lax.scan(backward_run, (zeros, zeros), (jnp.arange(N_ST, dtype=jnp.int32), by_run(query_blocks), by_run(event_blocks), by_run(event_grad_blocks), by_run(event_delta), by_run(partner), by_run(live)))
    key_sum = key_sum[BLK_DEV:BLK_DEV + EBLOCKS]
    value_sum = value_sum[BLK_DEV:BLK_DEV + EBLOCKS]
    grad_queries = grad_q.reshape(TOKENS, width)
    grad_event_values = grad_v.reshape(TOKENS, width)
    grad_keys = key_sum.reshape(TOKENS, width).astype(jnp.bfloat16)
    grad_frame_values = value_sum.reshape(TOKENS, width).astype(jnp.bfloat16)
    return (event_out, frame_out, grad_queries, grad_event_values, grad_keys, grad_frame_values)
```

```python
import jax
import jax.numpy as jnp
from jax import lax
from jax.experimental import pallas as pl
from jax.experimental.pallas import tpu as pltpu
from jax.sharding import PartitionSpec as P

DH = 64
BLOCK = 256
SLOTS = 3
HEADS = 4
FEATS = HEADS * DH
ROWS = 2 * BLOCK
PAIR = 2 * DH
EPS = 1e-06
NEG = -1e30
LOG2E = 1.4426950408889634
SCALE = DH**-0.5

KEYS, FVALS, QUERIES, EVALS, CODES = 0, ROWS, 2 * ROWS, 3 * ROWS, 4 * ROWS
MSG1 = 4 * ROWS + 16
STATS = 2 * ROWS
MSG2 = 2 * ROWS + 4 * 32

F32 = jnp.float32
BF16 = jnp.bfloat16
VMEM_LIMIT = 48 * 1024 * 1024


def dot(a, b):
    return jnp.dot(a, b, preferred_element_type=F32)


def params(**more):
    return pltpu.CompilerParams(vmem_limit_bytes=VMEM_LIMIT, **more)


def cost(flops):
    return pl.CostEstimate(flops=int(flops), bytes_accessed=1 << 20, transcendentals=0)


def neighbours(run):
    odd = lax.rem(run, 2)
    return run + 1 - 2 * odd, run - 1 + 2 * odd


def code_for(partner, live, run):
    code = jnp.int32(0)
    for a in range(2):
        for s in range(SLOTS):
            block = partner[a, s] - 2 * run
            hit = (s < live[a]) & (block >= 0) & (block < 2)
            code += jnp.where(hit, jnp.left_shift(1, 2 * a + jnp.clip(block, 0, 1)), 0)
    return code


def pair_list(todo, partner, live, sources):
    run = lax.axis_index("st")
    count = jnp.int32(0)

    def add(count, hit, self_block, place, block):
        todo[count] = self_block * 8 + place * 2 + block
        return count + hit.astype(jnp.int32)

    for place, (target, code) in enumerate(sources):
        for a in range(2):
            for s in range(SLOTS):
                block = partner[a, s] - 2 * target
                hit = (s < live[a]) & (block >= 0) & (block < 2)
                count = add(count, hit, a, place, block)
                if code is None:
                    count = add(count, hit, 2 + block, place, a)
            if code is not None:
                for f in range(2):
                    hit = jnp.bitwise_and(jnp.right_shift(code, 2 * a + f), 1) == 1
                    count = add(count, hit, 2 + f, place, a)
    return count


def read_code(rows, half):
    part = rows[:, half * PAIR : (half + 1) * PAIR].astype(F32)
    return jnp.max(part).astype(jnp.int32)


def masked(features_first, head):
    low = (head // 2) * PAIR
    tile = features_first[low : low + PAIR, :]
    row = lax.broadcasted_iota(jnp.int32, tile.shape, 0)
    return jnp.where(row // DH == head % 2, tile, jnp.zeros_like(tile))


def pack_kernel(partner, live, queries, event_values, keys, frame_values, msg):
    run = lax.axis_index("st")
    inner, outer = neighbours(run)
    msg[KEYS : KEYS + ROWS, :] = keys[...]
    msg[FVALS : FVALS + ROWS, :] = frame_values[...]
    msg[QUERIES : QUERIES + ROWS, :] = queries[...]
    msg[EVALS : EVALS + ROWS, :] = event_values[...]
    for half, target in enumerate((inner, outer)):
        code = code_for(partner, live, target).astype(F32)
        msg[CODES:MSG1, half * PAIR : (half + 1) * PAIR] = jnp.full((16, PAIR), code, F32).astype(BF16)


def attend(buf, vals_t, self_a, soft, acc, todo, count):
    def pair(n, _):
        entry = todo[n]
        me = lax.div(entry, 8)
        side = lax.div(me, 2)
        place = lax.div(lax.rem(entry, 8), 2)
        block = lax.rem(entry, 2)
        row = pl.multiple_of(side * (2 * ROWS) + block * BLOCK, BLOCK)
        at = place * 4 + side * 2 + block
        for h in range(HEADS):
            low = (h // 2) * PAIR
            other = buf[place, pl.ds(row, BLOCK), low : low + PAIR]
            scores = dot(other, self_a[me, h]) * LOG2E
            old_top = soft[me, h : h + 1, :]
            top = jnp.maximum(old_top, jnp.max(scores, axis=0, keepdims=True))
            weights = jnp.exp2(scores - top)
            decay = jnp.exp2(old_top - top)
            soft[me, h : h + 1, :] = top
            soft[me, HEADS + h : HEADS + h + 1, :] = soft[
                me, HEADS + h : HEADS + h + 1, :
            ] * decay + jnp.sum(weights, axis=0, keepdims=True)
            got = dot(vals_t[at, h * DH : (h + 1) * DH, :], weights.astype(BF16))
            acc[me, h * DH : (h + 1) * DH, :] = acc[me, h * DH : (h + 1) * DH, :] * decay + got
        return 0

    lax.fori_loop(0, count, pair, 0)


def other_values(buf, vals_t, place):
    for side, base in ((0, FVALS), (1, EVALS)):
        for block in range(2):
            low = base + block * BLOCK
            vals_t[place * 4 + side * 2 + block] = buf[place, low : low + BLOCK, :].T


def near_forward(
    partner, live, own, near, event_cot, frame_cot, self_a, self_v, cot_t, soft, acc, buf, vals_t, todo, sems
):
    copies = [pltpu.make_async_copy(src, buf.at[i], sems.at[i]) for i, src in enumerate((own, near))]
    for c in copies:
        c.start()
    for c in copies:
        c.wait()
    for side, (base_a, base_v) in enumerate(((QUERIES, EVALS), (KEYS, FVALS))):
        for block in range(2):
            me = side * 2 + block
            low = block * BLOCK
            a_t = buf[0, base_a + low : base_a + low + BLOCK, :].T * BF16(SCALE)
            v_t = buf[0, base_v + low : base_v + low + BLOCK, :].T
            for h in range(HEADS):
                self_a[me, h] = masked(a_t, h)
                self_v[me, h] = masked(v_t, h)
            cot = (event_cot, frame_cot)[side]
            cot_t[me] = cot[low : low + BLOCK, :].T
            soft[me, 0:HEADS, :] = jnp.full((HEADS, BLOCK), NEG, F32)
            soft[me, HEADS : 2 * HEADS, :] = jnp.zeros((HEADS, BLOCK), F32)
            acc[me] = jnp.zeros((FEATS, BLOCK), F32)
    other_values(buf, vals_t, 0)
    other_values(buf, vals_t, 1)
    run = lax.axis_index("st")
    inner, _ = neighbours(run)
    code = read_code(buf[1, CODES:MSG1, :], 0)
    count = pair_list(todo, partner, live, ((run, None), (inner, code)))
    attend(buf, vals_t, self_a, soft, acc, todo, count)


def far_forward(
    partner, live, far, self_a, cot_t, soft_in, acc_in, att, lse, sums, buf, soft, acc, vals_t, todo, sems
):
    copies = [
        pltpu.make_async_copy(far, buf.at[0], sems.at[0]),
        pltpu.make_async_copy(soft_in, soft, sems.at[1]),
        pltpu.make_async_copy(acc_in, acc, sems.at[2]),
    ]
    for c in copies:
        c.start()
    for c in copies:
        c.wait()
    other_values(buf, vals_t, 0)
    run = lax.axis_index("st")
    _, outer = neighbours(run)
    code = read_code(buf[0, CODES:MSG1, :], 1)
    count = pair_list(todo, partner, live, ((outer, code),))
    attend(buf, vals_t, self_a, soft, acc, todo, count)
    for me in range(4):
        square = jnp.zeros((1, BLOCK), F32)
        slope = jnp.zeros((1, BLOCK), F32)
        for h in range(HEADS):
            total = soft[me, HEADS + h : HEADS + h + 1, :]
            lse[me, h : h + 1, :] = soft[me, h : h + 1, :] + jnp.log2(total)
            part = acc[me, h * DH : (h + 1) * DH, :] * (1.0 / total)
            att[me, h * DH : (h + 1) * DH, :] = part
            square += jnp.sum(part * part, axis=0, keepdims=True)
            cot = cot_t[me, h * DH : (h + 1) * DH, :].astype(F32)
            slope += jnp.sum(part * cot, axis=0, keepdims=True)
        lse[me, HEADS : 2 * HEADS, :] = jnp.zeros((HEADS, BLOCK), F32)
        sums[2 * me : 2 * me + 1, :] = square
        sums[2 * me + 1 : 2 * me + 2, :] = slope


def split(value):
    high = value.astype(BF16).astype(F32)
    rest = value - high
    middle = rest.astype(BF16).astype(F32)
    return high, middle, rest - middle


def grad_kernel(width, att, cot_t, lse, sums, grad_t, normed_t, stats, msg):
    for me in range(4):
        rms = lax.rsqrt(sums[2 * me : 2 * me + 1, :] / width + EPS)
        slope = rms * sums[2 * me + 1 : 2 * me + 2, :] / width
        values = att[me]
        normed = values * rms
        grad = (rms * (cot_t[me].astype(F32) - normed * slope)).astype(BF16)
        grad_t[me] = grad
        normed_t[me] = normed.astype(BF16)
        low = ROWS * (1 - me // 2) + (me % 2) * BLOCK
        msg[low : low + BLOCK, :] = grad.T
        product = grad.astype(F32) * values
        deltas = [
            jnp.sum(product[h * DH : (h + 1) * DH, :], axis=0, keepdims=True) for h in range(HEADS)
        ]
        mine = jnp.concatenate([lse[me, 0:HEADS, :]] + deltas, axis=0)
        stats[me] = mine
        rows = jnp.concatenate(split(mine) + (jnp.zeros_like(mine),), axis=0)
        at = STATS + 32 * (2 * (1 - me // 2) + me % 2)
        msg[at : at + 32, :] = rows.astype(BF16)


def other_grads(buf1, buf2, a_t, g_t, columns, place):
    for side, base in ((0, KEYS), (1, QUERIES)):
        for block in range(2):
            at = place * 4 + side * 2 + block
            low = block * BLOCK
            a_t[at] = buf1[place, base + low : base + low + BLOCK, :].T
            low += side * ROWS
            g_t[at] = buf2[place, low : low + BLOCK, :].T
            low = STATS + 32 * (side * 2 + block)
            rows = buf2[place, low : low + 32, :].astype(F32)
            whole = rows[0:8, :] + rows[8:16, :] + rows[16:24, :]
            padded = jnp.concatenate([whole, jnp.zeros((PAIR - 8, BLOCK), F32)], axis=0)
            columns[at] = padded.T


def back(buf1, buf2, a_t, g_t, columns, self_a, self_v, self_g, stats, grad_a, grad_v, todo, count):
    def pair(n, _):
        entry = todo[n]
        me = lax.div(entry, 8)
        side = lax.div(me, 2)
        place = lax.div(lax.rem(entry, 8), 2)
        block = lax.rem(entry, 2)
        row_a = pl.multiple_of(side * (2 * ROWS) + block * BLOCK, BLOCK)
        row_v = pl.multiple_of(side * (2 * ROWS) + ROWS + block * BLOCK, BLOCK)
        row_g = pl.multiple_of(side * ROWS + block * BLOCK, BLOCK)
        at = place * 4 + side * 2 + block
        for h in range(HEADS):
            low = (h // 2) * PAIR
            lanes = slice(low, low + PAIR)
            head = slice(h * DH, (h + 1) * DH)
            scores = dot(buf1[place, pl.ds(row_a, BLOCK), lanes], self_a[me, h]) * LOG2E
            self_p = jnp.exp2(scores - stats[me, h : h + 1, :])
            other_p = jnp.exp2(scores - columns[at, :, h : h + 1])
            self_change = dot(buf1[place, pl.ds(row_v, BLOCK), lanes], self_g[me, h])
            other_change = dot(buf2[place, pl.ds(row_g, BLOCK), lanes], self_v[me, h])
            slope = self_p * (self_change - stats[me, HEADS + h : HEADS + h + 1, :]) + other_p * (
                other_change - columns[at, :, HEADS + h : HEADS + h + 1]
            )
            grad_a[me, head, :] += dot(a_t[at, head, :], slope.astype(BF16))
            grad_v[me, head, :] += dot(g_t[at, head, :], other_p.astype(BF16))
        return 0

    lax.fori_loop(0, count, pair, 0)


def near_backward(
    partner,
    live,
    own1,
    near1,
    own2,
    near2,
    self_a,
    self_v,
    grad_t,
    normed_t,
    stats,
    event_out,
    frame_out,
    self_g,
    grad_a,
    grad_v,
    buf1,
    buf2,
    a_t,
    g_t,
    columns,
    todo,
    sems,
):
    copies = [
        pltpu.make_async_copy(own1, buf1.at[0], sems.at[0]),
        pltpu.make_async_copy(near1, buf1.at[1], sems.at[1]),
        pltpu.make_async_copy(own2, buf2.at[0], sems.at[2]),
        pltpu.make_async_copy(near2, buf2.at[1], sems.at[3]),
    ]
    for c in copies:
        c.start()
    for me in range(4):
        out = (event_out, frame_out)[me // 2]
        low = (me % 2) * BLOCK
        out[low : low + BLOCK, :] = normed_t[me].T
        for h in range(HEADS):
            self_g[me, h] = masked(grad_t[me], h)
        grad_a[me] = jnp.zeros((FEATS, BLOCK), F32)
        grad_v[me] = jnp.zeros((FEATS, BLOCK), F32)
    for c in copies:
        c.wait()
    other_grads(buf1, buf2, a_t, g_t, columns, 0)
    other_grads(buf1, buf2, a_t, g_t, columns, 1)
    run = lax.axis_index("st")
    inner, _ = neighbours(run)
    code = read_code(buf1[1, CODES:MSG1, :], 0)
    count = pair_list(todo, partner, live, ((run, None), (inner, code)))
    back(buf1, buf2, a_t, g_t, columns, self_a, self_v, self_g, stats, grad_a, grad_v, todo, count)


def far_backward(
    partner,
    live,
    far1,
    far2,
    self_a,
    self_v,
    self_g,
    stats,
    grad_a_in,
    grad_v_in,
    grad_queries,
    grad_event_values,
    grad_keys,
    grad_frame_values,
    buf1,
    buf2,
    grad_a,
    grad_v,
    a_t,
    g_t,
    columns,
    todo,
    sems,
):
    copies = [
        pltpu.make_async_copy(far1, buf1.at[0], sems.at[0]),
        pltpu.make_async_copy(far2, buf2.at[0], sems.at[1]),
        pltpu.make_async_copy(grad_a_in, grad_a, sems.at[2]),
        pltpu.make_async_copy(grad_v_in, grad_v, sems.at[3]),
    ]
    for c in copies:
        c.start()
    for c in copies:
        c.wait()
    other_grads(buf1, buf2, a_t, g_t, columns, 0)
    run = lax.axis_index("st")
    _, outer = neighbours(run)
    code = read_code(buf1[0, CODES:MSG1, :], 1)
    count = pair_list(todo, partner, live, ((outer, code),))
    back(buf1, buf2, a_t, g_t, columns, self_a, self_v, self_g, stats, grad_a, grad_v, todo, count)
    for me in range(4):
        low = (me % 2) * BLOCK
        out_a, out_v = ((grad_queries, grad_event_values), (grad_keys, grad_frame_values))[me // 2]
        out_a[low : low + BLOCK, :] = (grad_a[me] * SCALE).astype(BF16).T
        out_v[low : low + BLOCK, :] = grad_v[me].astype(BF16).T


def shape(*dims, dtype=F32):
    return jax.ShapeDtypeStruct(dims, dtype)


def specs(*kinds):
    space = {"s": pltpu.SMEM, "v": pltpu.VMEM, "h": pl.ANY}
    return [pl.BlockSpec(memory_space=space[k]) for k in "".join(kinds)]


def on_device(
    event_queries,
    event_values,
    frame_keys,
    frame_values,
    partner,
    live_count,
    event_cotangent,
    frame_cotangent,
):
    width = FEATS * lax.axis_size("hd")
    runs = lax.axis_size("st")
    inner_pairs = [(i, i ^ 1) for i in range(runs)]
    outer_pairs = [(i, i + 1) for i in range(1, runs - 1, 2)] + [(i + 1, i) for i in range(1, runs - 1, 2)]
    tile = (4, FEATS, BLOCK)
    wide = (4, HEADS, PAIR, BLOCK)
    todo = pltpu.SMEM((40,), jnp.int32)

    msg = pl.pallas_call(
        pack_kernel,
        out_shape=shape(MSG1, FEATS, dtype=BF16),
        in_specs=specs("ssvvvv"),
        out_specs=specs("v")[0],
        compiler_params=params(),
    )(partner, live_count, event_queries, event_values, frame_keys, frame_values)
    far = lax.ppermute(msg, "st", outer_pairs)
    near = lax.ppermute(msg, "st", inner_pairs)

    self_a, self_v, cot_t, soft, acc = pl.pallas_call(
        near_forward,
        out_shape=(
            shape(*wide, dtype=BF16),
            shape(*wide, dtype=BF16),
            shape(*tile, dtype=BF16),
            shape(4, 2 * HEADS, BLOCK),
            shape(*tile),
        ),
        in_specs=specs("sshhvv"),
        out_specs=tuple(specs("vvvvv")),
        scratch_shapes=[
            pltpu.VMEM((2, MSG1, FEATS), BF16),
            pltpu.VMEM((8, FEATS, BLOCK), BF16),
            todo,
            pltpu.SemaphoreType.DMA((2,)),
        ],
        compiler_params=params(),
        cost_estimate=cost(5e9),
    )(partner, live_count, msg, near, event_cotangent, frame_cotangent)

    att, lse, sums = pl.pallas_call(
        far_forward,
        out_shape=(shape(*tile), shape(4, 2 * HEADS, BLOCK), shape(8, BLOCK)),
        in_specs=specs("sshvvhh"),
        out_specs=tuple(specs("vvv")),
        scratch_shapes=[
            pltpu.VMEM((1, MSG1, FEATS), BF16),
            pltpu.VMEM((4, 2 * HEADS, BLOCK), F32),
            pltpu.VMEM(tile, F32),
            pltpu.VMEM((4, FEATS, BLOCK), BF16),
            todo,
            pltpu.SemaphoreType.DMA((3,)),
        ],
        compiler_params=params(),
        cost_estimate=cost(3e9),
    )(partner, live_count, far, self_a, cot_t, soft, acc)
    sums = lax.psum(sums, "hd")

    grad_t, normed_t, stats, msg2 = pl.pallas_call(
        lambda *refs: grad_kernel(width, *refs),
        out_shape=(
            shape(*tile, dtype=BF16),
            shape(*tile, dtype=BF16),
            shape(4, 2 * HEADS, BLOCK),
            shape(MSG2, FEATS, dtype=BF16),
        ),
        in_specs=specs("vvvv"),
        out_specs=tuple(specs("vvvv")),
        compiler_params=params(),
        cost_estimate=cost(1e9),
    )(att, cot_t, lse, sums)
    far2 = lax.ppermute(msg2, "st", outer_pairs)
    near2 = lax.ppermute(msg2, "st", inner_pairs)

    event_out, frame_out, self_g, grad_a, grad_v = pl.pallas_call(
        near_backward,
        out_shape=(
            shape(ROWS, FEATS, dtype=BF16),
            shape(ROWS, FEATS, dtype=BF16),
            shape(*wide, dtype=BF16),
            shape(*tile),
            shape(*tile),
        ),
        in_specs=specs("sshhhhvvvvv"),
        out_specs=tuple(specs("vvvvv")),
        scratch_shapes=[
            pltpu.VMEM((2, MSG1, FEATS), BF16),
            pltpu.VMEM((2, MSG2, FEATS), BF16),
            pltpu.VMEM((8, FEATS, BLOCK), BF16),
            pltpu.VMEM((8, FEATS, BLOCK), BF16),
            pltpu.VMEM((8, BLOCK, PAIR), F32),
            todo,
            pltpu.SemaphoreType.DMA((4,)),
        ],
        compiler_params=params(),
        cost_estimate=cost(8e9),
    )(partner, live_count, msg, near, msg2, near2, self_a, self_v, grad_t, normed_t, stats)

    grads = pl.pallas_call(
        far_backward,
        out_shape=tuple(shape(ROWS, FEATS, dtype=BF16) for _ in range(4)),
        in_specs=specs("sshhvvvvhh"),
        out_specs=tuple(specs("vvvv")),
        scratch_shapes=[
            pltpu.VMEM((1, MSG1, FEATS), BF16),
            pltpu.VMEM((1, MSG2, FEATS), BF16),
            pltpu.VMEM(tile, F32),
            pltpu.VMEM(tile, F32),
            pltpu.VMEM((4, FEATS, BLOCK), BF16),
            pltpu.VMEM((4, FEATS, BLOCK), BF16),
            pltpu.VMEM((4, BLOCK, PAIR), F32),
            todo,
            pltpu.SemaphoreType.DMA((4,)),
        ],
        compiler_params=params(),
        cost_estimate=cost(6e9),
    )(partner, live_count, far, far2, self_a, self_v, self_g, stats, grad_a, grad_v)
    return (event_out, frame_out) + tuple(grads)


def solution(mesh):
    tokens = P("st", "hd")
    return jax.shard_map(
        on_device,
        mesh=mesh,
        in_specs=(tokens, tokens, tokens, tokens, P("st", None), P("st"), tokens, tokens),
        out_specs=(tokens,) * 6,
        check_vma=False,
    )
```

```python
import jax
import jax.numpy as jnp
from jax import lax
from jax.experimental import pallas as pl
from jax.experimental.pallas import tpu as pltpu
from jax.sharding import PartitionSpec as P

DH = 64
BLOCK = 256
SLOTS = 3
HEADS = 4
FEATS = HEADS * DH
ROWS = 2 * BLOCK
PAIR = 2 * DH
EPS = 1e-06
NEG = -1e30
LOG2E = 1.4426950408889634
SCALE = DH**-0.5

KEYS, FVALS, QUERIES, EVALS, CODES = 0, ROWS, 2 * ROWS, 3 * ROWS, 4 * ROWS
MSG1 = 4 * ROWS + 16
FAR1 = MSG1 + 16
STATS = 2 * ROWS
MSG2 = 2 * ROWS + 4 * 32
FAR2 = MSG2 + 16

F32 = jnp.float32
BF16 = jnp.bfloat16
VMEM_LIMIT = 32 * 1024 * 1024
PACK_LIMIT = 62 * 1024 * 1024


def dot(a, b):
    return jnp.dot(a, b, preferred_element_type=F32)


def dot_other_way(a, b):
    return lax.dot_general(a, b, (((1,), (1,)), ((), ())), preferred_element_type=F32)


def params(limit=VMEM_LIMIT, **more):
    return pltpu.CompilerParams(vmem_limit_bytes=limit, **more)


def cost(flops):
    return pl.CostEstimate(flops=int(flops), bytes_accessed=1 << 10, transcendentals=0)


def lanes(head):
    return slice((head // 2) * PAIR, (head // 2 + 1) * PAIR)


def feats(head):
    return slice(head * DH, (head + 1) * DH)


def stacked(parts):
    return jnp.concatenate(parts, axis=0)


def start_all(*copies):
    made = [pltpu.make_async_copy(*c) for c in copies]
    for c in made:
        c.start()
    return made


def code_for(partner, live, run):
    code = jnp.int32(0)
    for a in range(2):
        for s in range(SLOTS):
            block = partner[a, s] - 2 * run
            hit = (s < live[a]) & (block >= 0) & (block < 2)
            code += jnp.where(hit, jnp.left_shift(1, 2 * a + jnp.clip(block, 0, 1)), 0)
    return code


def bits(code):
    return [
        (a, f, jnp.bitwise_and(jnp.right_shift(code, 2 * a + f), 1)) for a in range(2) for f in range(2)
    ]


def pair_list(todo, as_events, as_frames):
    count = jnp.int32(0)
    for a, f, hit in bits(as_events):
        todo[count] = a * 2 + f
        count += hit
    for a, f, hit in bits(as_frames):
        todo[count] = (2 + f) * 2 + a
        count += hit
    return count


def read_code(msg, half):
    part = msg[CODES:MSG1, half * PAIR : (half + 1) * PAIR].astype(F32)
    return jnp.max(part).astype(jnp.int32)


def masked(features_first, head):
    tile = features_first[lanes(head), :]
    row = lax.broadcasted_iota(jnp.int32, tile.shape, 0)
    return jnp.where(row // DH == head % 2, tile, jnp.zeros_like(tile))


def pack_kernel(partner_in, live_in, queries, event_values, keys, frame_values, near, far, plan, partner, live, sems):
    parts = ((keys, KEYS), (frame_values, FVALS), (queries, QUERIES), (event_values, EVALS))
    tables = start_all((partner_in, partner, sems.at[0]), (live_in, live, sems.at[1]))
    arrays = start_all(*((part, far.at[low : low + ROWS], sems.at[2 + i]) for i, (part, low) in enumerate(parts)))
    for c in tables:
        c.wait()
    run = lax.axis_index("st")
    odd = lax.rem(run, 2)
    plan[0] = code_for(partner, live, run)
    for half, target in enumerate((run + 1 - 2 * odd, run - 1 + 2 * odd)):
        code = code_for(partner, live, target)
        plan[1 + half] = code
        far[CODES:FAR1, half * PAIR : (half + 1) * PAIR] = jnp.full(
            (32, PAIR), code.astype(F32), F32
        ).astype(BF16)
    for c in arrays:
        c.wait()
    near[...] = far[0:MSG1, :]


def attend(msg, vals_t, self_a, soft, acc, ahead, todo, count):
    def place(n):
        entry = todo[n]
        me = lax.div(entry, 2)
        side = lax.div(me, 2)
        block = lax.rem(entry, 2)
        return me, side * 2 + block, pl.multiple_of(side * (2 * ROWS) + block * BLOCK, BLOCK)

    def scores_of(n):
        me, _, row = place(n)
        return [dot(msg[pl.ds(row, BLOCK), lanes(h)], self_a[me, h]) for h in range(HEADS)]

    def keep(scores):
        for h in range(HEADS):
            ahead[h] = scores[h]

    keep(scores_of(0))

    def pair(n, _):
        me, at, _ = place(n)
        old, whole = soft[me], acc[me]
        scores = [ahead[h] for h in range(HEADS)]
        following = scores_of(jnp.minimum(n + 1, jnp.maximum(count - 1, 0)))
        tops, totals, decays, weights = [], [], [], []
        for h in range(HEADS):
            top = jnp.maximum(old[h : h + 1], jnp.max(scores[h], axis=0, keepdims=True))
            decay = jnp.exp(old[h : h + 1] - top)
            expo = jnp.exp(scores[h] - top)
            tops.append(top)
            decays.append(decay)
            totals.append(old[HEADS + h : HEADS + h + 1] * decay + jnp.sum(expo, axis=0, keepdims=True))
            weights.append(expo.astype(BF16))
        acc[me] = stacked(
            [whole[feats(h)] * decays[h] + dot(vals_t[at, feats(h), :], weights[h]) for h in range(HEADS)]
        )
        soft[me] = stacked(tops + totals)
        keep(following)
        return 0

    lax.fori_loop(0, count, pair, 0)


def other_values(msg, vals_t):
    for side, base in ((0, FVALS), (1, EVALS)):
        for block in range(2):
            low = base + block * BLOCK
            vals_t[side * 2 + block] = msg[low : low + BLOCK, :].T


def other_queries(msg, a_t):
    for side, base in ((0, KEYS), (1, QUERIES)):
        for block in range(2):
            low = base + block * BLOCK
            a_t[side * 2 + block] = msg[low : low + BLOCK, :].T * BF16(SCALE)


def near_forward(
    plan,
    own,
    near,
    event_cot,
    frame_cot,
    self_a,
    self_v,
    cot_t,
    soft,
    acc,
    near_a_t,
    cots,
    own_vals,
    near_vals,
    ahead,
    todo,
    sems,
):
    fetched = start_all((event_cot, cots.at[0], sems.at[0]), (frame_cot, cots.at[1], sems.at[1]))
    for side, (base_a, base_v) in enumerate(((QUERIES, EVALS), (KEYS, FVALS))):
        for block in range(2):
            me = side * 2 + block
            low = block * BLOCK
            a_t = own[base_a + low : base_a + low + BLOCK, :].T * BF16(SCALE)
            v_t = own[base_v + low : base_v + low + BLOCK, :].T
            own_vals[(1 - side) * 2 + block] = v_t
            for h in range(HEADS):
                self_a[me, h] = masked(a_t, h)
                self_v[me, h] = masked(v_t, h)
            soft[me, 0:HEADS, :] = jnp.full((HEADS, BLOCK), NEG, F32)
            soft[me, HEADS : 2 * HEADS, :] = jnp.zeros((HEADS, BLOCK), F32)
            acc[me] = jnp.zeros((FEATS, BLOCK), F32)
    count = pair_list(todo, plan[0], plan[0])
    attend(own, own_vals, self_a, soft, acc, ahead, todo, count)
    other_values(near, near_vals)
    count = pair_list(todo, plan[1], read_code(near, 0))
    attend(near, near_vals, self_a, soft, acc, ahead, todo, count)
    other_queries(near, near_a_t)
    for c in fetched:
        c.wait()
    for me in range(4):
        low = (me % 2) * BLOCK
        cot_t[me] = cots[me // 2, low : low + BLOCK, :].T


def far_forward(plan, far, self_a, cot_t, soft_in, acc_in, att, lse, sums, soft, vals_t, ahead, todo):
    acc = att
    soft[...] = soft_in[...]
    acc[...] = acc_in[...]
    other_values(far, vals_t)
    count = pair_list(todo, plan[2], read_code(far, 1))
    attend(far, vals_t, self_a, soft, acc, ahead, todo, count)
    for me in range(4):
        old, whole = soft[me], acc[me]
        total = old[HEADS : 2 * HEADS]
        lse[me] = stacked([old[0:HEADS] * LOG2E + jnp.log2(total), jnp.zeros((HEADS, BLOCK), F32)])
        inverse = 1.0 / total
        values = stacked([whole[feats(h)] * inverse[h : h + 1] for h in range(HEADS)])
        att[me] = values
        square = jnp.sum(values * values, axis=0, keepdims=True)
        slope = jnp.sum(values * cot_t[me].astype(F32), axis=0, keepdims=True)
        for to in range(sums.shape[0]):
            sums[to, 2 * me : 2 * me + 1, :] = square
            sums[to, 2 * me + 1 : 2 * me + 2, :] = slope


def split(value):
    high = value.astype(BF16).astype(F32)
    rest = value - high
    middle = rest.astype(BF16).astype(F32)
    return high, middle, rest - middle


def grad_kernel(width, att, cot_t, lse, sums, grad_t, normed_t, stats, msg, far):
    whole = jnp.sum(sums[...], axis=0)
    for me in range(4):
        rms = lax.rsqrt(whole[2 * me : 2 * me + 1, :] / width + EPS)
        slope = rms * whole[2 * me + 1 : 2 * me + 2, :] / width
        values = att[me]
        normed = values * rms
        grad = (rms * (cot_t[me].astype(F32) - normed * slope)).astype(BF16)
        grad_t[me] = grad
        normed_t[me] = normed.astype(BF16)
        side, block = 1 - me // 2, me % 2
        low = side * ROWS + block * BLOCK
        turned = grad.T
        msg[low : low + BLOCK, :] = turned
        far[low : low + BLOCK, :] = turned
        product = grad.astype(F32) * values
        deltas = [jnp.sum(product[feats(h)], axis=0, keepdims=True) for h in range(HEADS)]
        mine = stacked([lse[me, 0:HEADS, :]] + deltas)
        stats[me] = mine
        at = STATS + 32 * (2 * side + block)
        rows = stacked(split(mine) + (jnp.zeros_like(mine),)).astype(BF16)
        msg[at : at + 32, :] = rows
        far[at : at + 32, :] = rows
    far[MSG2:FAR2, :] = jnp.zeros((16, FEATS), BF16)


def as_columns(rows):
    return stacked([rows, jnp.zeros((PAIR - 2 * HEADS, BLOCK), F32)]).T


def other_grads(msg, g_t, columns):
    for side in range(2):
        for block in range(2):
            low = side * ROWS + block * BLOCK
            g_t[side * 2 + block] = msg[low : low + BLOCK, :].T
            low = STATS + 32 * (side * 2 + block)
            rows = msg[low : low + 32, :].astype(F32)
            columns[side * 2 + block] = as_columns(rows[0:8] + rows[8:16] + rows[16:24])


def in_order(dots, weigh, outs):
    dots(0)
    dots(1)
    dots(2)
    weigh(0)
    dots(3)
    for h in range(HEADS):
        outs(h)
        if h + 1 < HEADS:
            weigh(h + 1)


def slopes(made, row_stats, columns, h):
    scores, self_change, other_change = made
    scores = scores * LOG2E
    self_p = jnp.exp2(scores - row_stats[h : h + 1])
    other_p = jnp.exp2(scores - columns[:, h : h + 1])
    g = HEADS + h
    slope = self_p * (self_change - row_stats[g : g + 1]) + other_p * (other_change - columns[:, g : g + 1])
    return slope.astype(BF16), self_p.astype(BF16), other_p.astype(BF16)


def back(msg1, msg2, a_t, g_t, columns, self_a, self_v, self_g, stats, grad_a, grad_v, todo, count):
    def pair(n, _):
        entry = todo[n]
        me = lax.div(entry, 2)
        side = lax.div(me, 2)
        block = lax.rem(entry, 2)
        row_a = pl.multiple_of(side * (2 * ROWS) + block * BLOCK, BLOCK)
        row_v = pl.multiple_of(side * (2 * ROWS) + ROWS + block * BLOCK, BLOCK)
        row_g = pl.multiple_of(side * ROWS + block * BLOCK, BLOCK)
        at = side * 2 + block
        mine, theirs = stats[me], columns[at]
        made, ready, sums = {}, {}, {}

        def dots(h):
            made[h] = (
                dot(msg1[pl.ds(row_a, BLOCK), lanes(h)], self_a[me, h]),
                dot(msg1[pl.ds(row_v, BLOCK), lanes(h)], self_g[me, h]),
                dot(msg2[pl.ds(row_g, BLOCK), lanes(h)], self_v[me, h]),
            )

        def weigh(h):
            ready[h] = slopes(made[h], mine, theirs, h)

        def outs(h):
            slope, _, other_p = ready[h]
            sums[h] = dot(a_t[at, feats(h), :], slope), dot(g_t[at, feats(h), :], other_p)

        in_order(dots, weigh, outs)
        grad_a[me] += stacked([sums[h][0] for h in range(HEADS)])
        grad_v[me] += stacked([sums[h][1] for h in range(HEADS)])
        return 0

    lax.fori_loop(0, count, pair, 0)


def back_own(msg1, msg2, columns, self_a, self_v, self_g, grad_t, stats, grad_a, grad_v, todo, count):
    def pair(n, _):
        entry = todo[n]
        me = lax.div(entry, 2)
        block = lax.rem(entry, 2)
        frame = 2 + block
        row_a = pl.multiple_of(KEYS + block * BLOCK, BLOCK)
        row_v = pl.multiple_of(FVALS + block * BLOCK, BLOCK)
        row_g = pl.multiple_of(block * BLOCK, BLOCK)
        mine, theirs = stats[me], columns[block]
        made, ready, sums = {}, {}, {}

        def dots(h):
            made[h] = (
                dot(msg1[pl.ds(row_a, BLOCK), lanes(h)], self_a[me, h]),
                dot(msg1[pl.ds(row_v, BLOCK), lanes(h)], self_g[me, h]),
                dot(msg2[pl.ds(row_g, BLOCK), lanes(h)], self_v[me, h]),
            )

        def weigh(h):
            ready[h] = slopes(made[h], mine, theirs, h)

        def outs(h):
            slope, self_p, other_p = ready[h]
            half = slice((h % 2) * DH, (h % 2 + 1) * DH)
            sums[h] = (
                dot(self_a[frame, h, half, :], slope),
                dot(grad_t[frame, feats(h), :], other_p),
                dot_other_way(self_a[me, h, half, :], slope),
                dot_other_way(grad_t[me, feats(h), :], self_p),
            )

        in_order(dots, weigh, outs)
        grad_a[me] += stacked([sums[h][0] for h in range(HEADS)])
        grad_v[me] += stacked([sums[h][1] for h in range(HEADS)])
        grad_a[frame] += stacked([sums[h][2] for h in range(HEADS)])
        grad_v[frame] += stacked([sums[h][3] for h in range(HEADS)])
        return 0

    lax.fori_loop(0, count, pair, 0)


def own_backward(
    plan, own1, own2, self_a, self_v, grad_t, stats, self_g, grad_a, grad_v, columns, todo
):
    for me in range(4):
        for h in range(HEADS):
            self_g[me, h] = masked(grad_t[me], h)
        grad_a[me] = jnp.zeros((FEATS, BLOCK), F32)
        grad_v[me] = jnp.zeros((FEATS, BLOCK), F32)
    for block in range(2):
        columns[block] = as_columns(stats[2 + block])
    count = pair_list(todo, plan[0], jnp.int32(0))
    back_own(own1, own2, columns, self_a, self_v, self_g, grad_t, stats, grad_a, grad_v, todo, count)


def send_grads(me, grad_a, grad_v, ready, outs, sems):
    side, low = me // 2, (me % 2) * BLOCK
    copies = []
    for k, grad in enumerate((grad_a, grad_v)):
        ready[2 * me + k] = grad[me].astype(BF16).T
        copies += start_all((ready.at[2 * me + k], outs[2 * side + k].at[low : low + BLOCK], sems.at[2 * me + k]))
    return copies


def near_backward(
    plan,
    near1,
    far1,
    near2,
    self_a,
    self_v,
    self_g,
    near_a_t,
    normed_t,
    stats,
    grad_a_in,
    grad_v_in,
    grad_a,
    grad_v,
    event_out,
    frame_out,
    grad_queries,
    grad_event_values,
    grad_keys,
    grad_frame_values,
    far_a_t,
    g_t,
    columns,
    ready,
    todo,
    sems,
):
    grad_a[...] = grad_a_in[...]
    grad_v[...] = grad_v_in[...]
    other_grads(near2, g_t, columns)
    count = pair_list(todo, plan[1], read_code(near1, 0))
    back(near1, near2, near_a_t, g_t, columns, self_a, self_v, self_g, stats, grad_a, grad_v, todo, count)
    outs = (grad_queries, grad_event_values, grad_keys, grad_frame_values)
    copies = []
    for me in range(4):
        copies += send_grads(me, grad_a, grad_v, ready, outs, sems)
        low = (me % 2) * BLOCK
        ready[8 + me] = normed_t[me].T
        copies += start_all(
            (ready.at[8 + me], (event_out, frame_out)[me // 2].at[low : low + BLOCK], sems.at[8 + me])
        )
    other_queries(far1, far_a_t)
    for c in copies:
        c.wait()


def far_backward(
    plan,
    far1,
    far2,
    self_a,
    self_v,
    self_g,
    far_a_t,
    stats,
    grad_a_in,
    grad_v_in,
    _queries,
    _event_values,
    _keys,
    _frame_values,
    grad_queries,
    grad_event_values,
    grad_keys,
    grad_frame_values,
    grad_a,
    grad_v,
    g_t,
    columns,
    ready,
    todo,
    sems,
):
    code = read_code(far1, 1)
    touched = [jnp.bitwise_and(plan[2], 3 * 4**a) != 0 for a in range(2)] + [
        jnp.bitwise_and(code, 5 * 2**f) != 0 for f in range(2)
    ]
    outs = (grad_queries, grad_event_values, grad_keys, grad_frame_values)
    count = pair_list(todo, plan[2], code)

    @pl.when(count > 0)
    def _():
        for me in range(4):

            @pl.when(touched[me])
            def _():
                grad_a[me] = grad_a_in[me]
                grad_v[me] = grad_v_in[me]

        other_grads(far2, g_t, columns)
        back(far1, far2, far_a_t, g_t, columns, self_a, self_v, self_g, stats, grad_a, grad_v, todo, count)
        for me in range(4):

            @pl.when(touched[me])
            def _():
                send_grads(me, grad_a, grad_v, ready, outs, sems)

        for me in range(4):

            @pl.when(touched[me])
            def _():
                side, low = me // 2, (me % 2) * BLOCK
                for k in range(2):
                    pltpu.make_async_copy(
                        ready.at[2 * me + k], outs[2 * side + k].at[low : low + BLOCK], sems.at[2 * me + k]
                    ).wait()


def shape(*dims, dtype=F32):
    return jax.ShapeDtypeStruct(dims, dtype)


def specs(kinds):
    space = {"s": pltpu.SMEM, "v": pltpu.VMEM, "h": pltpu.HBM}
    return [pl.BlockSpec(memory_space=space[k]) for k in kinds]


def kernel(body, operands, places, outs, out_places, scratch=(), flops=0, limit=VMEM_LIMIT, aliases=()):
    return pl.pallas_call(
        body,
        out_shape=tuple(outs),
        in_specs=specs(places),
        out_specs=tuple(specs(out_places)),
        scratch_shapes=list(scratch),
        compiler_params=params(limit),
        cost_estimate=cost(flops),
        input_output_aliases=dict(aliases),
    )(*operands)


def on_device(
    event_queries,
    event_values,
    frame_keys,
    frame_values,
    partner,
    live_count,
    event_cotangent,
    frame_cotangent,
):
    width = FEATS * lax.axis_size("hd")
    runs = lax.axis_size("st")
    inner_pairs = [(i, i ^ 1) for i in range(runs)]
    outer_pairs = [(i, i + 1) for i in range(1, runs - 1, 2)] + [(i + 1, i) for i in range(1, runs - 1, 2)]
    tile = (4, FEATS, BLOCK)
    wide = (4, HEADS, PAIR, BLOCK)
    small = (4, 2 * HEADS, BLOCK)
    todo = pltpu.SMEM((16,), jnp.int32)

    msg1, far_msg1, plan = kernel(
        pack_kernel,
        (partner, live_count, event_queries, event_values, frame_keys, frame_values),
        "hhhhhh",
        (shape(MSG1, FEATS, dtype=BF16), shape(FAR1, FEATS, dtype=BF16), shape(8, dtype=jnp.int32)),
        "vvs",
        [
            pltpu.SMEM((2, SLOTS), jnp.int32),
            pltpu.SMEM((2,), jnp.int32),
            pltpu.SemaphoreType.DMA((6,)),
        ],
        limit=PACK_LIMIT,
    )
    far1 = lax.ppermute(far_msg1, "st", outer_pairs)
    near1 = lax.ppermute(msg1, "st", inner_pairs)

    self_a, self_v, cot_t, soft, acc, near_a_t = kernel(
        near_forward,
        (plan, msg1, near1, event_cotangent, frame_cotangent),
        "svvhh",
        (
            shape(*wide, dtype=BF16),
            shape(*wide, dtype=BF16),
            shape(*tile, dtype=BF16),
            shape(*small),
            shape(*tile),
            shape(*tile, dtype=BF16),
        ),
        "vvvvvv",
        [
            pltpu.VMEM((2, ROWS, FEATS), BF16),
            pltpu.VMEM(tile, BF16),
            pltpu.VMEM(tile, BF16),
            pltpu.VMEM((HEADS, BLOCK, BLOCK), F32),
            todo,
            pltpu.SemaphoreType.DMA((2,)),
        ],
        1e6,
    )
    att, lse, sums = kernel(
        far_forward,
        (plan, far1, self_a, cot_t, soft, acc),
        "svvvvv",
        (shape(*tile), shape(*small), shape(lax.axis_size("hd"), 8, BLOCK)),
        "vvv",
        [
            pltpu.VMEM(small, F32),
            pltpu.VMEM(tile, BF16),
            pltpu.VMEM((HEADS, BLOCK, BLOCK), F32),
            todo,
        ],
        1e6,
    )
    sums = lax.all_to_all(sums, "hd", 0, 0)

    grad_t, normed_t, stats, msg2, far_msg2 = kernel(
        lambda *refs: grad_kernel(width, *refs),
        (att, cot_t, lse, sums),
        "vvvv",
        (
            shape(*tile, dtype=BF16),
            shape(*tile, dtype=BF16),
            shape(*small),
            shape(MSG2, FEATS, dtype=BF16),
            shape(FAR2, FEATS, dtype=BF16),
        ),
        "vvvvv",
        flops=1e6,
    )
    far2 = lax.ppermute(far_msg2, "st", outer_pairs)
    near2 = lax.ppermute(msg2, "st", inner_pairs)

    self_g, grad_a, grad_v = kernel(
        own_backward,
        (plan, msg1, msg2, self_a, self_v, grad_t, stats),
        "svvvvvv",
        (shape(*wide, dtype=BF16), shape(*tile), shape(*tile)),
        "vvv",
        [pltpu.VMEM((2, BLOCK, PAIR), F32), todo],
        1e6,
    )
    whole = [shape(ROWS, FEATS, dtype=BF16)]
    grad_a, grad_v, event_out, frame_out, *grads, far_a_t = kernel(
        near_backward,
        (plan, near1, far1, near2, self_a, self_v, self_g, near_a_t, normed_t, stats, grad_a, grad_v),
        "svvvvvvvvvvv",
        [shape(*tile)] * 2 + whole * 6 + [shape(*tile, dtype=BF16)],
        "vvhhhhhhv",
        [
            pltpu.VMEM(tile, BF16),
            pltpu.VMEM((4, BLOCK, PAIR), F32),
            pltpu.VMEM((12, BLOCK, FEATS), BF16),
            todo,
            pltpu.SemaphoreType.DMA((12,)),
        ],
        1e6,
    )
    grads = kernel(
        far_backward,
        (plan, far1, far2, self_a, self_v, self_g, far_a_t, stats, grad_a, grad_v, *grads),
        "svvvvvvvvvhhhh",
        whole * 4,
        "hhhh",
        [
            pltpu.VMEM(tile, F32),
            pltpu.VMEM(tile, F32),
            pltpu.VMEM(tile, BF16),
            pltpu.VMEM((4, BLOCK, PAIR), F32),
            pltpu.VMEM((8, BLOCK, FEATS), BF16),
            todo,
            pltpu.SemaphoreType.DMA((8,)),
        ],
        1e6,
        aliases=((10, 0), (11, 1), (12, 2), (13, 3)),
    )
    return (event_out, frame_out) + tuple(grads)


def solution(mesh):
    tokens = P("st", "hd")
    return jax.shard_map(
        on_device,
        mesh=mesh,
        in_specs=(tokens, tokens, tokens, tokens, P("st", None), P("st"), tokens, tokens),
        out_specs=(tokens,) * 6,
        check_vma=False,
    )
```

```python
import jax
import jax.numpy as jnp
from jax import lax
from jax.experimental import pallas as pl
from jax.experimental.pallas import tpu as pltpu
from jax.sharding import PartitionSpec as P

DH = 64
BLOCK = 256
SLOTS = 3
HEADS = 4
FEATS = HEADS * DH
ROWS = 2 * BLOCK
PAIR = 2 * DH
EPS = 1e-06
NEG = -1e30
LOG2E = 1.4426950408889634
SCALE = DH**-0.5

KEYS, FVALS, QUERIES, EVALS, CODES = 0, ROWS, 2 * ROWS, 3 * ROWS, 4 * ROWS
MSG1 = 4 * ROWS + 16
FAR1 = MSG1 + 16
STATS = 2 * ROWS
MSG2 = 2 * ROWS + 4 * 32
FAR2 = MSG2 + 16
KEPT = 3

F32 = jnp.float32
BF16 = jnp.bfloat16
VMEM_LIMIT = 32 * 1024 * 1024
PACK_LIMIT = 62 * 1024 * 1024


def dot(a, b):
    return jnp.dot(a, b, preferred_element_type=F32)


def dot_other_way(a, b):
    return lax.dot_general(a, b, (((1,), (1,)), ((), ())), preferred_element_type=F32)


def params(limit=VMEM_LIMIT, **more):
    return pltpu.CompilerParams(vmem_limit_bytes=limit, **more)


def cost(flops):
    return pl.CostEstimate(flops=int(flops), bytes_accessed=1 << 10, transcendentals=0)


def lanes(head):
    return slice((head // 2) * PAIR, (head // 2 + 1) * PAIR)


def feats(head):
    return slice(head * DH, (head + 1) * DH)


def stacked(parts):
    return jnp.concatenate(parts, axis=0)


def start_all(*copies):
    made = [pltpu.make_async_copy(*c) for c in copies]
    for c in made:
        c.start()
    return made


def code_for(partner, live, run):
    code = jnp.int32(0)
    for a in range(2):
        for s in range(SLOTS):
            block = partner[a, s] - 2 * run
            hit = (s < live[a]) & (block >= 0) & (block < 2)
            code += jnp.where(hit, jnp.left_shift(1, 2 * a + jnp.clip(block, 0, 1)), 0)
    return code


def bits(code):
    return [
        (a, f, jnp.bitwise_and(jnp.right_shift(code, 2 * a + f), 1)) for a in range(2) for f in range(2)
    ]


def pair_list(todo, as_events, as_frames):
    count = jnp.int32(0)
    for a, f, hit in bits(as_events):
        todo[count] = a * 2 + f
        count += hit
    for a, f, hit in bits(as_frames):
        todo[count] = (2 + f) * 2 + a
        count += hit
    return count


def read_code(msg, half):
    part = msg[CODES:MSG1, half * PAIR : (half + 1) * PAIR].astype(F32)
    return jnp.max(part).astype(jnp.int32)


def masked(features_first, head):
    tile = features_first[lanes(head), :]
    row = lax.broadcasted_iota(jnp.int32, tile.shape, 0)
    return jnp.where(row // DH == head % 2, tile, jnp.zeros_like(tile))


def pack_kernel(partner_in, live_in, queries, event_values, keys, frame_values, msg, plan, partner, live, sems):
    parts = ((keys, KEYS), (frame_values, FVALS), (queries, QUERIES), (event_values, EVALS))
    tables = start_all((partner_in, partner, sems.at[0]), (live_in, live, sems.at[1]))
    arrays = start_all(*((part, msg.at[low : low + ROWS], sems.at[2 + i]) for i, (part, low) in enumerate(parts)))
    for c in tables:
        c.wait()
    run = lax.axis_index("st")
    odd = lax.rem(run, 2)
    plan[0] = code_for(partner, live, run)
    for half, target in enumerate((run + 1 - 2 * odd, run - 1 + 2 * odd)):
        code = code_for(partner, live, target)
        plan[1 + half] = code
        msg[CODES:FAR1, half * PAIR : (half + 1) * PAIR] = jnp.full((32, PAIR), code.astype(F32), F32).astype(BF16)
    for c in arrays:
        c.wait()


def attend(msg, vals_t, self_a, soft, acc, ahead, todo, count):
    def place(n):
        entry = todo[n]
        me = lax.div(entry, 2)
        side = lax.div(me, 2)
        block = lax.rem(entry, 2)
        return me, side * 2 + block, pl.multiple_of(side * (2 * ROWS) + block * BLOCK, BLOCK)

    def scores_of(n):
        me, _, row = place(n)
        return [dot(msg[pl.ds(row, BLOCK), lanes(h)], self_a[me, h]) for h in range(HEADS)]

    def keep(scores):
        for h in range(HEADS):
            ahead[h] = scores[h]

    keep(scores_of(0))

    def pair(n, _):
        me, at, _ = place(n)
        old, whole = soft[me], acc[me]
        scores = [ahead[h] for h in range(HEADS)]
        following = scores_of(jnp.minimum(n + 1, jnp.maximum(count - 1, 0)))
        tops, totals, decays, weights = [], [], [], []
        for h in range(HEADS):
            top = jnp.maximum(old[h : h + 1], jnp.max(scores[h], axis=0, keepdims=True))
            decay = jnp.exp(old[h : h + 1] - top)
            expo = jnp.exp(scores[h] - top)
            tops.append(top)
            decays.append(decay)
            totals.append(old[HEADS + h : HEADS + h + 1] * decay + jnp.sum(expo, axis=0, keepdims=True))
            weights.append(expo.astype(BF16))
        acc[me] = stacked(
            [whole[feats(h)] * decays[h] + dot(vals_t[at, feats(h), :], weights[h]) for h in range(HEADS)]
        )
        soft[me] = stacked(tops + totals)
        keep(following)
        return 0

    lax.fori_loop(0, count, pair, 0)


def other_values(msg, vals_t):
    for side, base in ((0, FVALS), (1, EVALS)):
        for block in range(2):
            low = base + block * BLOCK
            vals_t[side * 2 + block] = msg[low : low + BLOCK, :].T


def other_queries(msg, a_t):
    for side, base in ((0, KEYS), (1, QUERIES)):
        for block in range(2):
            low = base + block * BLOCK
            a_t[side * 2 + block] = msg[low : low + BLOCK, :].T * BF16(SCALE)


def near_forward(
    plan,
    own,
    near,
    event_cot,
    frame_cot,
    self_a,
    self_v,
    cot_t,
    soft,
    acc,
    near_a_t,
    cots,
    own_vals,
    near_vals,
    ahead,
    todo,
    sems,
):
    fetched = start_all((event_cot, cots.at[0], sems.at[0]), (frame_cot, cots.at[1], sems.at[1]))
    for side, (base_a, base_v) in enumerate(((QUERIES, EVALS), (KEYS, FVALS))):
        for block in range(2):
            me = side * 2 + block
            low = block * BLOCK
            a_t = own[base_a + low : base_a + low + BLOCK, :].T * BF16(SCALE)
            v_t = own[base_v + low : base_v + low + BLOCK, :].T
            own_vals[(1 - side) * 2 + block] = v_t
            for h in range(HEADS):
                self_a[me, h] = masked(a_t, h)
                self_v[me, h] = masked(v_t, h)
            soft[me, 0:HEADS, :] = jnp.full((HEADS, BLOCK), NEG, F32)
            soft[me, HEADS : 2 * HEADS, :] = jnp.zeros((HEADS, BLOCK), F32)
            acc[me] = jnp.zeros((FEATS, BLOCK), F32)
    count = pair_list(todo, plan[0], plan[0])
    attend(own, own_vals, self_a, soft, acc, ahead, todo, count)
    other_values(near, near_vals)
    count = pair_list(todo, plan[1], read_code(near, 0))
    attend(near, near_vals, self_a, soft, acc, ahead, todo, count)
    other_queries(near, near_a_t)
    for c in fetched:
        c.wait()
    for me in range(4):
        low = (me % 2) * BLOCK
        cot_t[me] = cots[me // 2, low : low + BLOCK, :].T


def far_forward(plan, far, self_a, cot_t, soft_in, acc_in, att, lse, sums, soft, vals_t, ahead, todo):
    acc = att
    soft[...] = soft_in[...]
    acc[...] = acc_in[...]
    other_values(far, vals_t)
    count = pair_list(todo, plan[2], read_code(far, 1))
    attend(far, vals_t, self_a, soft, acc, ahead, todo, count)
    for me in range(4):
        old, whole = soft[me], acc[me]
        total = old[HEADS : 2 * HEADS]
        lse[me] = stacked([old[0:HEADS] * LOG2E + jnp.log2(total), jnp.zeros((HEADS, BLOCK), F32)])
        inverse = 1.0 / total
        values = stacked([whole[feats(h)] * inverse[h : h + 1] for h in range(HEADS)])
        att[me] = values
        square = jnp.sum(values * values, axis=0, keepdims=True)
        slope = jnp.sum(values * cot_t[me].astype(F32), axis=0, keepdims=True)
        for to in range(sums.shape[0]):
            sums[to, 2 * me : 2 * me + 1, :] = square
            sums[to, 2 * me + 1 : 2 * me + 2, :] = slope


def split(value):
    high = value.astype(BF16).astype(F32)
    rest = value - high
    middle = rest.astype(BF16).astype(F32)
    return high, middle, rest - middle


def grad_kernel(width, att, cot_t, lse, sums, grad_t, normed_t, stats, msg, far):
    whole = jnp.sum(sums[...], axis=0)
    for me in range(4):
        rms = lax.rsqrt(whole[2 * me : 2 * me + 1, :] / width + EPS)
        slope = rms * whole[2 * me + 1 : 2 * me + 2, :] / width
        values = att[me]
        normed = values * rms
        grad = (rms * (cot_t[me].astype(F32) - normed * slope)).astype(BF16)
        grad_t[me] = grad
        normed_t[me] = normed.astype(BF16)
        side, block = 1 - me // 2, me % 2
        low = side * ROWS + block * BLOCK
        turned = grad.T
        msg[low : low + BLOCK, :] = turned
        far[low : low + BLOCK, :] = turned
        product = grad.astype(F32) * values
        deltas = [jnp.sum(product[feats(h)], axis=0, keepdims=True) for h in range(HEADS)]
        mine = stacked([lse[me, 0:HEADS, :]] + deltas)
        stats[me] = mine
        at = STATS + 32 * (2 * side + block)
        rows = stacked(split(mine) + (jnp.zeros_like(mine),)).astype(BF16)
        msg[at : at + 32, :] = rows
        far[at : at + 32, :] = rows
    far[MSG2:FAR2, :] = jnp.zeros((16, FEATS), BF16)


def as_columns(rows):
    return stacked([rows, jnp.zeros((PAIR - 2 * HEADS, BLOCK), F32)]).T


def other_grads(msg, g_t, columns):
    for side in range(2):
        for block in range(2):
            low = side * ROWS + block * BLOCK
            g_t[side * 2 + block] = msg[low : low + BLOCK, :].T
            low = STATS + 32 * (side * 2 + block)
            rows = msg[low : low + 32, :].astype(F32)
            columns[side * 2 + block] = as_columns(rows[0:8] + rows[8:16] + rows[16:24])


def in_order(dots, weigh, outs):
    dots(0)
    dots(1)
    dots(2)
    weigh(0)
    dots(3)
    for h in range(HEADS):
        outs(h)
        if h + 1 < HEADS:
            weigh(h + 1)


def slopes(made, row_stats, columns, h):
    scores, self_change, other_change = made
    scores = scores * LOG2E
    self_p = jnp.exp2(scores - row_stats[h : h + 1])
    other_p = jnp.exp2(scores - columns[:, h : h + 1])
    g = HEADS + h
    slope = self_p * (self_change - row_stats[g : g + 1]) + other_p * (other_change - columns[:, g : g + 1])
    return slope.astype(BF16), self_p.astype(BF16), other_p.astype(BF16)


def back(msg1, msg2, a_t, g_t, columns, self_a, self_v, self_g, stats, grad_a, grad_v, todo, count, first=0):
    def pair(n, _):
        entry = todo[n]
        me = lax.div(entry, 2)
        side = lax.div(me, 2)
        block = lax.rem(entry, 2)
        row_a = pl.multiple_of(side * (2 * ROWS) + block * BLOCK, BLOCK)
        row_v = pl.multiple_of(side * (2 * ROWS) + ROWS + block * BLOCK, BLOCK)
        row_g = pl.multiple_of(side * ROWS + block * BLOCK, BLOCK)
        at = side * 2 + block
        mine, theirs = stats[me], columns[at]
        made, ready, sums = {}, {}, {}

        def dots(h):
            made[h] = (
                dot(msg1[pl.ds(row_a, BLOCK), lanes(h)], self_a[me, h]),
                dot(msg1[pl.ds(row_v, BLOCK), lanes(h)], self_g[me, h]),
                dot(msg2[pl.ds(row_g, BLOCK), lanes(h)], self_v[me, h]),
            )

        def weigh(h):
            ready[h] = slopes(made[h], mine, theirs, h)

        def outs(h):
            slope, _, other_p = ready[h]
            sums[h] = dot(a_t[at, feats(h), :], slope), dot(g_t[at, feats(h), :], other_p)

        in_order(dots, weigh, outs)
        grad_a[me] += stacked([sums[h][0] for h in range(HEADS)])
        grad_v[me] += stacked([sums[h][1] for h in range(HEADS)])
        return 0

    lax.fori_loop(first, count, pair, 0)


def part_way(msg1, self_a, self_g, stats, kept_scores, kept_terms, todo, count):
    def pair(n, _):
        entry = todo[n]
        me = lax.div(entry, 2)
        side = lax.div(me, 2)
        block = lax.rem(entry, 2)
        row_a = pl.multiple_of(side * (2 * ROWS) + block * BLOCK, BLOCK)
        row_v = pl.multiple_of(side * (2 * ROWS) + ROWS + block * BLOCK, BLOCK)
        mine = stats[me]
        scores = [dot(msg1[pl.ds(row_a, BLOCK), lanes(h)], self_a[me, h]) * LOG2E for h in range(HEADS)]
        changes = [dot(msg1[pl.ds(row_v, BLOCK), lanes(h)], self_g[me, h]) for h in range(HEADS)]
        for h in range(HEADS):
            g = HEADS + h
            kept_scores[n, h] = scores[h]
            kept_terms[n, h] = jnp.exp2(scores[h] - mine[h : h + 1]) * (changes[h] - mine[g : g + 1])
        return 0

    lax.fori_loop(0, count, pair, 0)


def back_rest(msg2, a_t, g_t, columns, self_v, kept_scores, kept_terms, grad_a, grad_v, todo, count):
    def pair(n, _):
        entry = todo[n]
        me = lax.div(entry, 2)
        side = lax.div(me, 2)
        block = lax.rem(entry, 2)
        row_g = pl.multiple_of(side * ROWS + block * BLOCK, BLOCK)
        at = side * 2 + block
        theirs = columns[at]
        made, ready, sums = {}, {}, {}

        def dots(h):
            made[h] = dot(msg2[pl.ds(row_g, BLOCK), lanes(h)], self_v[me, h])

        def weigh(h):
            g = HEADS + h
            other_p = jnp.exp2(kept_scores[n, h] - theirs[:, h : h + 1])
            slope = kept_terms[n, h] + other_p * (made[h] - theirs[:, g : g + 1])
            ready[h] = slope.astype(BF16), other_p.astype(BF16)

        def outs(h):
            slope, other_p = ready[h]
            sums[h] = dot(a_t[at, feats(h), :], slope), dot(g_t[at, feats(h), :], other_p)

        in_order(dots, weigh, outs)
        grad_a[me] += stacked([sums[h][0] for h in range(HEADS)])
        grad_v[me] += stacked([sums[h][1] for h in range(HEADS)])
        return 0

    lax.fori_loop(0, count, pair, 0)


def back_own(msg1, msg2, columns, self_a, self_v, self_g, grad_t, stats, grad_a, grad_v, todo, count):
    def pair(n, _):
        entry = todo[n]
        me = lax.div(entry, 2)
        block = lax.rem(entry, 2)
        frame = 2 + block
        row_a = pl.multiple_of(KEYS + block * BLOCK, BLOCK)
        row_v = pl.multiple_of(FVALS + block * BLOCK, BLOCK)
        row_g = pl.multiple_of(block * BLOCK, BLOCK)
        mine, theirs = stats[me], columns[block]
        made, ready, sums = {}, {}, {}

        def dots(h):
            made[h] = (
                dot(msg1[pl.ds(row_a, BLOCK), lanes(h)], self_a[me, h]),
                dot(msg1[pl.ds(row_v, BLOCK), lanes(h)], self_g[me, h]),
                dot(msg2[pl.ds(row_g, BLOCK), lanes(h)], self_v[me, h]),
            )

        def weigh(h):
            ready[h] = slopes(made[h], mine, theirs, h)

        def outs(h):
            slope, self_p, other_p = ready[h]
            half = slice((h % 2) * DH, (h % 2 + 1) * DH)
            sums[h] = (
                dot(self_a[frame, h, half, :], slope),
                dot(grad_t[frame, feats(h), :], other_p),
                dot_other_way(self_a[me, h, half, :], slope),
                dot_other_way(grad_t[me, feats(h), :], self_p),
            )

        in_order(dots, weigh, outs)
        grad_a[me] += stacked([sums[h][0] for h in range(HEADS)])
        grad_v[me] += stacked([sums[h][1] for h in range(HEADS)])
        grad_a[frame] += stacked([sums[h][2] for h in range(HEADS)])
        grad_v[frame] += stacked([sums[h][3] for h in range(HEADS)])
        return 0

    lax.fori_loop(0, count, pair, 0)


def own_backward(
    plan, own1, own2, self_a, self_v, grad_t, stats, self_g, grad_a, grad_v, columns, todo
):
    for me in range(4):
        for h in range(HEADS):
            self_g[me, h] = masked(grad_t[me], h)
        grad_a[me] = jnp.zeros((FEATS, BLOCK), F32)
        grad_v[me] = jnp.zeros((FEATS, BLOCK), F32)
    for block in range(2):
        columns[block] = as_columns(stats[2 + block])
    count = pair_list(todo, plan[0], jnp.int32(0))
    back_own(own1, own2, columns, self_a, self_v, self_g, grad_t, stats, grad_a, grad_v, todo, count)


def send_grads(me, grad_a, grad_v, ready, outs, sems):
    side, low = me // 2, (me % 2) * BLOCK
    copies = []
    for k, grad in enumerate((grad_a, grad_v)):
        ready[2 * me + k] = grad[me].astype(BF16).T
        copies += start_all((ready.at[2 * me + k], outs[2 * side + k].at[low : low + BLOCK], sems.at[2 * me + k]))
    return copies


def near_backward(
    plan,
    near1,
    far1,
    near2,
    self_a,
    self_v,
    self_g,
    near_a_t,
    normed_t,
    stats,
    grad_a_in,
    grad_v_in,
    grad_a,
    grad_v,
    event_out,
    frame_out,
    grad_queries,
    grad_event_values,
    grad_keys,
    grad_frame_values,
    far_a_t,
    kept_scores,
    kept_terms,
    g_t,
    columns,
    ready,
    todo,
    sems,
):
    grad_a[...] = grad_a_in[...]
    grad_v[...] = grad_v_in[...]
    other_grads(near2, g_t, columns)
    count = pair_list(todo, plan[1], read_code(near1, 0))
    back(near1, near2, near_a_t, g_t, columns, self_a, self_v, self_g, stats, grad_a, grad_v, todo, count)
    outs = (grad_queries, grad_event_values, grad_keys, grad_frame_values)
    copies = []
    for me in range(4):
        copies += send_grads(me, grad_a, grad_v, ready, outs, sems)
        low = (me % 2) * BLOCK
        ready[8 + me] = normed_t[me].T
        copies += start_all(
            (ready.at[8 + me], (event_out, frame_out)[me // 2].at[low : low + BLOCK], sems.at[8 + me])
        )
    other_queries(far1, far_a_t)
    count = pair_list(todo, plan[2], read_code(far1, 1))
    part_way(far1, self_a, self_g, stats, kept_scores, kept_terms, todo, jnp.minimum(count, KEPT))
    for c in copies:
        c.wait()


def far_backward(
    plan,
    far1,
    far2,
    self_a,
    self_v,
    self_g,
    far_a_t,
    stats,
    kept_scores,
    kept_terms,
    grad_a_in,
    grad_v_in,
    _queries,
    _event_values,
    _keys,
    _frame_values,
    grad_queries,
    grad_event_values,
    grad_keys,
    grad_frame_values,
    grad_a,
    grad_v,
    g_t,
    columns,
    ready,
    todo,
    sems,
):
    code = read_code(far1, 1)
    touched = [jnp.bitwise_and(plan[2], 3 * 4**a) != 0 for a in range(2)] + [
        jnp.bitwise_and(code, 5 * 2**f) != 0 for f in range(2)
    ]
    outs = (grad_queries, grad_event_values, grad_keys, grad_frame_values)
    count = pair_list(todo, plan[2], code)

    @pl.when(count > 0)
    def _():
        for me in range(4):

            @pl.when(touched[me])
            def _():
                grad_a[me] = grad_a_in[me]
                grad_v[me] = grad_v_in[me]

        other_grads(far2, g_t, columns)
        begun = jnp.minimum(count, KEPT)
        back_rest(far2, far_a_t, g_t, columns, self_v, kept_scores, kept_terms, grad_a, grad_v, todo, begun)
        back(
            far1, far2, far_a_t, g_t, columns, self_a, self_v, self_g, stats, grad_a, grad_v, todo, count, begun
        )
        for me in range(4):

            @pl.when(touched[me])
            def _():
                send_grads(me, grad_a, grad_v, ready, outs, sems)

        for me in range(4):

            @pl.when(touched[me])
            def _():
                side, low = me // 2, (me % 2) * BLOCK
                for k in range(2):
                    pltpu.make_async_copy(
                        ready.at[2 * me + k], outs[2 * side + k].at[low : low + BLOCK], sems.at[2 * me + k]
                    ).wait()


def shape(*dims, dtype=F32):
    return jax.ShapeDtypeStruct(dims, dtype)


def specs(kinds):
    space = {"s": pltpu.SMEM, "v": pltpu.VMEM, "h": pltpu.HBM}
    return [pl.BlockSpec(memory_space=space[k]) for k in kinds]


def kernel(body, operands, places, outs, out_places, scratch=(), flops=0, limit=VMEM_LIMIT, aliases=()):
    return pl.pallas_call(
        body,
        out_shape=tuple(outs),
        in_specs=specs(places),
        out_specs=tuple(specs(out_places)),
        scratch_shapes=list(scratch),
        compiler_params=params(limit),
        cost_estimate=cost(flops),
        input_output_aliases=dict(aliases),
    )(*operands)


def on_device(
    event_queries,
    event_values,
    frame_keys,
    frame_values,
    partner,
    live_count,
    event_cotangent,
    frame_cotangent,
):
    width = FEATS * lax.axis_size("hd")
    runs = lax.axis_size("st")
    inner_pairs = [(i, i ^ 1) for i in range(runs)]
    outer_pairs = [(i, i + 1) for i in range(1, runs - 1, 2)] + [(i + 1, i) for i in range(1, runs - 1, 2)]
    tile = (4, FEATS, BLOCK)
    wide = (4, HEADS, PAIR, BLOCK)
    small = (4, 2 * HEADS, BLOCK)
    todo = pltpu.SMEM((16,), jnp.int32)

    far_msg1, plan = kernel(
        pack_kernel,
        (partner, live_count, event_queries, event_values, frame_keys, frame_values),
        "hhhhhh",
        (shape(FAR1, FEATS, dtype=BF16), shape(8, dtype=jnp.int32)),
        "vs",
        [
            pltpu.SMEM((2, SLOTS), jnp.int32),
            pltpu.SMEM((2,), jnp.int32),
            pltpu.SemaphoreType.DMA((6,)),
        ],
        limit=PACK_LIMIT,
    )
    far1 = lax.ppermute(far_msg1, "st", outer_pairs)
    msg1 = far_msg1[0:MSG1]
    near1 = lax.ppermute(msg1, "st", inner_pairs)

    self_a, self_v, cot_t, soft, acc, near_a_t = kernel(
        near_forward,
        (plan, msg1, near1, event_cotangent, frame_cotangent),
        "svvhh",
        (
            shape(*wide, dtype=BF16),
            shape(*wide, dtype=BF16),
            shape(*tile, dtype=BF16),
            shape(*small),
            shape(*tile),
            shape(*tile, dtype=BF16),
        ),
        "vvvvvv",
        [
            pltpu.VMEM((2, ROWS, FEATS), BF16),
            pltpu.VMEM(tile, BF16),
            pltpu.VMEM(tile, BF16),
            pltpu.VMEM((HEADS, BLOCK, BLOCK), F32),
            todo,
            pltpu.SemaphoreType.DMA((2,)),
        ],
        1e6,
    )
    att, lse, sums = kernel(
        far_forward,
        (plan, far1, self_a, cot_t, soft, acc),
        "svvvvv",
        (shape(*tile), shape(*small), shape(lax.axis_size("hd"), 8, BLOCK)),
        "vvv",
        [
            pltpu.VMEM(small, F32),
            pltpu.VMEM(tile, BF16),
            pltpu.VMEM((HEADS, BLOCK, BLOCK), F32),
            todo,
        ],
        1e6,
    )
    sums = lax.all_to_all(sums, "hd", 0, 0)

    grad_t, normed_t, stats, msg2, far_msg2 = kernel(
        lambda *refs: grad_kernel(width, *refs),
        (att, cot_t, lse, sums),
        "vvvv",
        (
            shape(*tile, dtype=BF16),
            shape(*tile, dtype=BF16),
            shape(*small),
            shape(MSG2, FEATS, dtype=BF16),
            shape(FAR2, FEATS, dtype=BF16),
        ),
        "vvvvv",
        flops=1e6,
    )
    far2 = lax.ppermute(far_msg2, "st", outer_pairs)
    near2 = lax.ppermute(msg2, "st", inner_pairs)

    self_g, grad_a, grad_v = kernel(
        own_backward,
        (plan, msg1, msg2, self_a, self_v, grad_t, stats),
        "svvvvvv",
        (shape(*wide, dtype=BF16), shape(*tile), shape(*tile)),
        "vvv",
        [pltpu.VMEM((2, BLOCK, PAIR), F32), todo],
        1e6,
    )
    whole = [shape(ROWS, FEATS, dtype=BF16)]
    grad_a, grad_v, event_out, frame_out, *grads, far_a_t, kept_scores, kept_terms = kernel(
        near_backward,
        (plan, near1, far1, near2, self_a, self_v, self_g, near_a_t, normed_t, stats, grad_a, grad_v),
        "svvvvvvvvvvv",
        [shape(*tile)] * 2 + whole * 6 + [shape(*tile, dtype=BF16)] + [shape(KEPT, HEADS, BLOCK, BLOCK)] * 2,
        "vvhhhhhhvvv",
        [
            pltpu.VMEM(tile, BF16),
            pltpu.VMEM((4, BLOCK, PAIR), F32),
            pltpu.VMEM((12, BLOCK, FEATS), BF16),
            todo,
            pltpu.SemaphoreType.DMA((12,)),
        ],
        1e6,
    )
    grads = kernel(
        far_backward,
        (plan, far1, far2, self_a, self_v, self_g, far_a_t, stats, kept_scores, kept_terms, grad_a, grad_v, *grads),
        "svvvvvvvvvvvhhhh",
        whole * 4,
        "hhhh",
        [
            pltpu.VMEM(tile, F32),
            pltpu.VMEM(tile, F32),
            pltpu.VMEM(tile, BF16),
            pltpu.VMEM((4, BLOCK, PAIR), F32),
            pltpu.VMEM((8, BLOCK, FEATS), BF16),
            todo,
            pltpu.SemaphoreType.DMA((8,)),
        ],
        1e6,
        aliases=((12, 0), (13, 1), (14, 2), (15, 3)),
    )
    return (event_out, frame_out) + tuple(grads)


def solution(mesh):
    tokens = P("st", "hd")
    return jax.shard_map(
        on_device,
        mesh=mesh,
        in_specs=(tokens, tokens, tokens, tokens, P("st", None), P("st"), tokens, tokens),
        out_specs=(tokens,) * 6,
        check_vma=False,
    )
```

```python
import jax
import jax.numpy as jnp
from jax import lax
from jax.experimental import pallas as pl
from jax.experimental.pallas import tpu as pltpu
from jax.sharding import PartitionSpec as P

DH = 64
BLOCK = 256
SLOTS = 3
HEADS = 4
FEATS = HEADS * DH
ROWS = 2 * BLOCK
PAIR = 2 * DH
EPS = 1e-06
NEG = -1e30
LOG2E = 1.4426950408889634
SCALE = DH**-0.5

KEYS, FVALS, QUERIES, EVALS, CODES = 0, ROWS, 2 * ROWS, 3 * ROWS, 4 * ROWS
MSG1 = 4 * ROWS + 16
FAR1 = MSG1 + 16
STATS = 2 * ROWS
MIDDLE = STATS + 4 * 8
LOW = MIDDLE + 4 * 8
MSG2 = LOW + 4 * 4
FAR2 = MSG2 + 16
KEPT = 3
HELD = 4

F32 = jnp.float32
BF16 = jnp.bfloat16
VMEM_LIMIT = 28 * 1024 * 1024
PACK_LIMIT = 62 * 1024 * 1024


def dot(a, b):
    return jnp.dot(a, b, preferred_element_type=F32)


def dot_other_way(a, b):
    return lax.dot_general(a, b, (((1,), (1,)), ((), ())), preferred_element_type=F32)


def params(limit=VMEM_LIMIT, **more):
    return pltpu.CompilerParams(vmem_limit_bytes=limit, **more)


def cost(flops):
    return pl.CostEstimate(flops=int(flops), bytes_accessed=1 << 10, transcendentals=0)


def lanes(head):
    return slice((head // 2) * PAIR, (head // 2 + 1) * PAIR)


def feats(head):
    return slice(head * DH, (head + 1) * DH)


def stacked(parts):
    return jnp.concatenate(parts, axis=0)


def start_all(*copies):
    made = [pltpu.make_async_copy(*c) for c in copies]
    for c in made:
        c.start()
    return made


def code_for(partner, live, run):
    code = jnp.int32(0)
    for a in range(2):
        for s in range(SLOTS):
            block = partner[a, s] - 2 * run
            hit = (s < live[a]) & (block >= 0) & (block < 2)
            code += jnp.where(hit, jnp.left_shift(1, 2 * a + jnp.clip(block, 0, 1)), 0)
    return code


def bits(code):
    return [
        (a, f, jnp.bitwise_and(jnp.right_shift(code, 2 * a + f), 1)) for a in range(2) for f in range(2)
    ]


def pair_list(todo, as_events, as_frames):
    count = jnp.int32(0)
    for a, f, hit in bits(as_events):
        todo[count] = a * 2 + f
        count += hit
    for a, f, hit in bits(as_frames):
        todo[count] = (2 + f) * 2 + a
        count += hit
    return count


def read_code(msg, half):
    part = msg[CODES:MSG1, half * PAIR : (half + 1) * PAIR].astype(F32)
    return jnp.max(part).astype(jnp.int32)


def masked(features_first, head):
    tile = features_first[lanes(head), :]
    row = lax.broadcasted_iota(jnp.int32, tile.shape, 0)
    return jnp.where(row // DH == head % 2, tile, jnp.zeros_like(tile))


def pack_kernel(partner_in, live_in, queries, event_values, keys, frame_values, msg, plan, partner, live, sems):
    parts = ((keys, KEYS), (frame_values, FVALS), (queries, QUERIES), (event_values, EVALS))
    tables = start_all((partner_in, partner, sems.at[0]), (live_in, live, sems.at[1]))
    arrays = start_all(*((part, msg.at[low : low + ROWS], sems.at[2 + i]) for i, (part, low) in enumerate(parts)))
    for c in tables:
        c.wait()
    run = lax.axis_index("st")
    odd = lax.rem(run, 2)
    plan[0] = code_for(partner, live, run)
    for half, target in enumerate((run + 1 - 2 * odd, run - 1 + 2 * odd)):
        code = code_for(partner, live, target)
        plan[1 + half] = code
        msg[CODES:FAR1, half * PAIR : (half + 1) * PAIR] = jnp.full((32, PAIR), code.astype(F32), F32).astype(BF16)
    for c in arrays:
        c.wait()


def attend(msg, vals_t, self_a, soft, acc, ahead, todo, count):
    slots = ahead.shape[0]

    def place(n):
        entry = todo[n]
        me = lax.div(entry, 2)
        side = lax.div(me, 2)
        block = lax.rem(entry, 2)
        return me, side * 2 + block, pl.multiple_of(side * (2 * ROWS) + block * BLOCK, BLOCK)

    def scores_of(n):
        me, _, row = place(n)
        return [dot(msg[pl.ds(row, BLOCK), lanes(h)], self_a[me, h]) for h in range(HEADS)]

    def keep(n, scores):
        slot = jnp.minimum(n, slots - 1)
        for h in range(HEADS):
            ahead[slot, h] = scores[h]

    keep(0, scores_of(0))

    def pair(n, _):
        me, at, _ = place(n)
        old, whole = soft[me], acc[me]
        slot = jnp.minimum(n, slots - 1)
        scores = [ahead[slot, h] for h in range(HEADS)]
        after = jnp.minimum(n + 1, count - 1)
        following = scores_of(after)
        tops, totals, decays, weights = [], [], [], []
        for h in range(HEADS):
            top = jnp.maximum(old[h : h + 1], jnp.max(scores[h], axis=0, keepdims=True))
            decay = jnp.exp(old[h : h + 1] - top)
            expo = jnp.exp(scores[h] - top)
            tops.append(top)
            decays.append(decay)
            totals.append(old[HEADS + h : HEADS + h + 1] * decay + jnp.sum(expo, axis=0, keepdims=True))
            weights.append(expo.astype(BF16))
        acc[me] = stacked(
            [whole[feats(h)] * decays[h] + dot(vals_t[at, feats(h), :], weights[h]) for h in range(HEADS)]
        )
        soft[me] = stacked(tops + totals)
        keep(after, following)
        return 0

    lax.fori_loop(0, count, pair, 0)


def other_values(msg, vals_t):
    for side, base in ((0, FVALS), (1, EVALS)):
        for block in range(2):
            low = base + block * BLOCK
            vals_t[side * 2 + block] = msg[low : low + BLOCK, :].T


def other_queries(msg, a_t):
    for side, base in ((0, KEYS), (1, QUERIES)):
        for block in range(2):
            low = base + block * BLOCK
            a_t[side * 2 + block] = msg[low : low + BLOCK, :].T * BF16(SCALE)


def near_forward(
    plan,
    own,
    near,
    event_cot,
    frame_cot,
    self_a,
    self_v,
    cot_t,
    soft,
    acc,
    near_a_t,
    own_scores,
    near_scores,
    cots,
    own_vals,
    near_vals,
    todo,
    sems,
):
    fetched = start_all((event_cot, cots.at[0], sems.at[0]), (frame_cot, cots.at[1], sems.at[1]))
    for side, (base_a, base_v) in enumerate(((QUERIES, EVALS), (KEYS, FVALS))):
        for block in range(2):
            me = side * 2 + block
            low = block * BLOCK
            a_t = own[base_a + low : base_a + low + BLOCK, :].T * BF16(SCALE)
            v_t = own[base_v + low : base_v + low + BLOCK, :].T
            own_vals[(1 - side) * 2 + block] = v_t
            for h in range(HEADS):
                self_a[me, h] = masked(a_t, h)
                self_v[me, h] = masked(v_t, h)
            soft[me, 0:HEADS, :] = jnp.full((HEADS, BLOCK), NEG, F32)
            soft[me, HEADS : 2 * HEADS, :] = jnp.zeros((HEADS, BLOCK), F32)
            acc[me] = jnp.zeros((FEATS, BLOCK), F32)
    count = pair_list(todo, plan[0], plan[0])
    attend(own, own_vals, self_a, soft, acc, own_scores, todo, count)
    other_values(near, near_vals)
    count = pair_list(todo, plan[1], read_code(near, 0))
    attend(near, near_vals, self_a, soft, acc, near_scores, todo, count)
    other_queries(near, near_a_t)
    for c in fetched:
        c.wait()
    for me in range(4):
        low = (me % 2) * BLOCK
        cot_t[me] = cots[me // 2, low : low + BLOCK, :].T


def far_forward(plan, far, self_a, cot_t, soft_in, acc_in, att, lse, sums, soft, vals_t, ahead, todo):
    acc = att
    soft[...] = soft_in[...]
    acc[...] = acc_in[...]
    other_values(far, vals_t)
    count = pair_list(todo, plan[2], read_code(far, 1))
    attend(far, vals_t, self_a, soft, acc, ahead, todo, count)
    for me in range(4):
        old, whole = soft[me], acc[me]
        total = old[HEADS : 2 * HEADS]
        lse[me] = stacked([old[0:HEADS] * LOG2E + jnp.log2(total), jnp.zeros((HEADS, BLOCK), F32)])
        inverse = 1.0 / total
        values = stacked([whole[feats(h)] * inverse[h : h + 1] for h in range(HEADS)])
        att[me] = values
        square = jnp.sum(values * values, axis=0, keepdims=True)
        slope = jnp.sum(values * cot_t[me].astype(F32), axis=0, keepdims=True)
        for to in range(sums.shape[0]):
            sums[to, 2 * me : 2 * me + 1, :] = square
            sums[to, 2 * me + 1 : 2 * me + 2, :] = slope


def split(value):
    high = value.astype(BF16).astype(F32)
    rest = value - high
    middle = rest.astype(BF16).astype(F32)
    return high, middle, rest - middle


def grad_kernel(width, att, cot_t, lse, sums, grad_t, normed_t, stats, msg, far):
    whole = jnp.sum(sums[...], axis=0)
    parts = {}
    for me in range(4):
        rms = lax.rsqrt(whole[2 * me : 2 * me + 1, :] / width + EPS)
        slope = rms * whole[2 * me + 1 : 2 * me + 2, :] / width
        values = att[me]
        normed = values * rms
        grad = (rms * (cot_t[me].astype(F32) - normed * slope)).astype(BF16)
        grad_t[me] = grad
        normed_t[me] = normed.astype(BF16)
        side, block = 1 - me // 2, me % 2
        low = side * ROWS + block * BLOCK
        turned = grad.T
        msg[low : low + BLOCK, :] = turned
        far[low : low + BLOCK, :] = turned
        product = grad.astype(F32) * values
        deltas = [jnp.sum(product[feats(h)], axis=0, keepdims=True) for h in range(HEADS)]
        mine = stacked([lse[me, 0:HEADS, :]] + deltas)
        stats[me] = mine
        parts[2 * side + block] = split(mine)
    rows = stacked(
        [parts[at][0] for at in range(4)]
        + [parts[at][1] for at in range(4)]
        + [parts[at][2][0:HEADS] for at in range(4)]
    ).astype(BF16)
    msg[STATS:MSG2, :] = rows
    far[STATS:MSG2, :] = rows
    far[MSG2:FAR2, :] = jnp.zeros((16, FEATS), BF16)


def as_columns(rows):
    return stacked([rows, jnp.zeros((PAIR - 2 * HEADS, BLOCK), F32)]).T


def other_grads(msg, g_t, columns):
    high = msg[STATS:MIDDLE, :].astype(F32) + msg[MIDDLE:LOW, :].astype(F32)
    rest = msg[LOW:MSG2, :].astype(F32)
    for at in range(4):
        g_t[at] = msg[at * BLOCK : (at + 1) * BLOCK, :].T
        whole = high[8 * at : 8 * at + 8]
        columns[at] = as_columns(stacked([whole[0:HEADS] + rest[4 * at : 4 * at + 4], whole[HEADS : 2 * HEADS]]))


def in_order(dots, weigh, outs):
    dots(0)
    dots(1)
    dots(2)
    weigh(0)
    dots(3)
    for h in range(HEADS):
        outs(h)
        if h + 1 < HEADS:
            weigh(h + 1)


def slopes(made, row_stats, columns, h):
    scores, self_change, other_change = made
    scores = scores * LOG2E
    self_p = jnp.exp2(scores - row_stats[h : h + 1])
    other_p = jnp.exp2(scores - columns[:, h : h + 1])
    g = HEADS + h
    slope = self_p * (self_change - row_stats[g : g + 1]) + other_p * (other_change - columns[:, g : g + 1])
    return slope.astype(BF16), self_p.astype(BF16), other_p.astype(BF16)


def back(
    msg1, msg2, a_t, g_t, columns, self_a, self_v, self_g, stats, grad_a, grad_v, todo, first, count, held=None
):
    def pair(n, _):
        entry = todo[n]
        me = lax.div(entry, 2)
        side = lax.div(me, 2)
        block = lax.rem(entry, 2)
        row_a = pl.multiple_of(side * (2 * ROWS) + block * BLOCK, BLOCK)
        row_v = pl.multiple_of(side * (2 * ROWS) + ROWS + block * BLOCK, BLOCK)
        row_g = pl.multiple_of(side * ROWS + block * BLOCK, BLOCK)
        at = side * 2 + block
        mine, theirs = stats[me], columns[at]
        made, ready, sums = {}, {}, {}

        def dots(h):
            made[h] = (
                dot(msg1[pl.ds(row_a, BLOCK), lanes(h)], self_a[me, h]) if held is None else held[n, h],
                dot(msg1[pl.ds(row_v, BLOCK), lanes(h)], self_g[me, h]),
                dot(msg2[pl.ds(row_g, BLOCK), lanes(h)], self_v[me, h]),
            )

        def weigh(h):
            ready[h] = slopes(made[h], mine, theirs, h)

        def outs(h):
            slope, _, other_p = ready[h]
            sums[h] = dot(a_t[at, feats(h), :], slope), dot(g_t[at, feats(h), :], other_p)

        in_order(dots, weigh, outs)
        grad_a[me] += stacked([sums[h][0] for h in range(HEADS)])
        grad_v[me] += stacked([sums[h][1] for h in range(HEADS)])
        return 0

    lax.fori_loop(first, count, pair, 0)


def part_way(msg1, self_a, self_g, stats, kept_scores, kept_terms, todo, count):
    def pair(n, _):
        entry = todo[n]
        me = lax.div(entry, 2)
        side = lax.div(me, 2)
        block = lax.rem(entry, 2)
        row_a = pl.multiple_of(side * (2 * ROWS) + block * BLOCK, BLOCK)
        row_v = pl.multiple_of(side * (2 * ROWS) + ROWS + block * BLOCK, BLOCK)
        mine = stats[me]
        scores = [dot(msg1[pl.ds(row_a, BLOCK), lanes(h)], self_a[me, h]) * LOG2E for h in range(HEADS)]
        changes = [dot(msg1[pl.ds(row_v, BLOCK), lanes(h)], self_g[me, h]) for h in range(HEADS)]
        for h in range(HEADS):
            g = HEADS + h
            kept_scores[n, h] = scores[h]
            kept_terms[n, h] = jnp.exp2(scores[h] - mine[h : h + 1]) * (changes[h] - mine[g : g + 1])
        return 0

    lax.fori_loop(0, count, pair, 0)


def back_rest(msg2, a_t, g_t, columns, self_v, kept_scores, kept_terms, grad_a, grad_v, todo, count):
    def pair(n, _):
        entry = todo[n]
        me = lax.div(entry, 2)
        side = lax.div(me, 2)
        block = lax.rem(entry, 2)
        row_g = pl.multiple_of(side * ROWS + block * BLOCK, BLOCK)
        at = side * 2 + block
        theirs = columns[at]
        made, ready, sums = {}, {}, {}

        def dots(h):
            made[h] = dot(msg2[pl.ds(row_g, BLOCK), lanes(h)], self_v[me, h])

        def weigh(h):
            g = HEADS + h
            other_p = jnp.exp2(kept_scores[n, h] - theirs[:, h : h + 1])
            slope = kept_terms[n, h] + other_p * (made[h] - theirs[:, g : g + 1])
            ready[h] = slope.astype(BF16), other_p.astype(BF16)

        def outs(h):
            slope, other_p = ready[h]
            sums[h] = dot(a_t[at, feats(h), :], slope), dot(g_t[at, feats(h), :], other_p)

        in_order(dots, weigh, outs)
        grad_a[me] += stacked([sums[h][0] for h in range(HEADS)])
        grad_v[me] += stacked([sums[h][1] for h in range(HEADS)])
        return 0

    lax.fori_loop(0, count, pair, 0)


def back_own(msg1, msg2, columns, self_a, self_v, self_g, grad_t, stats, held, grad_a, grad_v, todo, count):
    def pair(n, _):
        entry = todo[n]
        me = lax.div(entry, 2)
        block = lax.rem(entry, 2)
        frame = 2 + block
        row_v = pl.multiple_of(FVALS + block * BLOCK, BLOCK)
        row_g = pl.multiple_of(block * BLOCK, BLOCK)
        mine, theirs = stats[me], columns[block]
        made, ready, sums = {}, {}, {}

        def dots(h):
            made[h] = (
                held[n, h],
                dot(msg1[pl.ds(row_v, BLOCK), lanes(h)], self_g[me, h]),
                dot(msg2[pl.ds(row_g, BLOCK), lanes(h)], self_v[me, h]),
            )

        def weigh(h):
            ready[h] = slopes(made[h], mine, theirs, h)

        def outs(h):
            slope, self_p, other_p = ready[h]
            half = slice((h % 2) * DH, (h % 2 + 1) * DH)
            sums[h] = (
                dot(self_a[frame, h, half, :], slope),
                dot(grad_t[frame, feats(h), :], other_p),
                dot_other_way(self_a[me, h, half, :], slope),
                dot_other_way(grad_t[me, feats(h), :], self_p),
            )

        in_order(dots, weigh, outs)
        grad_a[me] += stacked([sums[h][0] for h in range(HEADS)])
        grad_v[me] += stacked([sums[h][1] for h in range(HEADS)])
        grad_a[frame] += stacked([sums[h][2] for h in range(HEADS)])
        grad_v[frame] += stacked([sums[h][3] for h in range(HEADS)])
        return 0

    lax.fori_loop(0, count, pair, 0)


def own_backward(
    plan, own1, own2, self_a, self_v, grad_t, stats, own_scores, self_g, grad_a, grad_v, columns, todo
):
    for me in range(4):
        for h in range(HEADS):
            self_g[me, h] = masked(grad_t[me], h)
        grad_a[me] = jnp.zeros((FEATS, BLOCK), F32)
        grad_v[me] = jnp.zeros((FEATS, BLOCK), F32)
    for block in range(2):
        columns[block] = as_columns(stats[2 + block])
    count = pair_list(todo, plan[0], jnp.int32(0))
    back_own(own1, own2, columns, self_a, self_v, self_g, grad_t, stats, own_scores, grad_a, grad_v, todo, count)


def touched_blocks(as_events, as_frames):
    return [jnp.bitwise_and(as_events, 3 * 4**a) != 0 for a in range(2)] + [
        jnp.bitwise_and(as_frames, 5 * 2**f) != 0 for f in range(2)
    ]


def wait_grads(me, ready, outs, sems):
    side, low = me // 2, (me % 2) * BLOCK
    for k in range(2):
        at = 2 * me + k
        pltpu.make_async_copy(ready.at[at], outs[2 * side + k].at[low : low + BLOCK], sems.at[at]).wait()


def send_grads(me, grad_a, grad_v, ready, outs, sems):
    side, low = me // 2, (me % 2) * BLOCK
    for k, grad in enumerate((grad_a, grad_v)):
        ready[2 * me + k] = grad[me].astype(BF16).T
        start_all((ready.at[2 * me + k], outs[2 * side + k].at[low : low + BLOCK], sems.at[2 * me + k]))


def near_backward(
    plan,
    near1,
    far1,
    near2,
    self_a,
    self_v,
    self_g,
    near_a_t,
    normed_t,
    stats,
    near_scores,
    grad_a_in,
    grad_v_in,
    grad_a,
    grad_v,
    event_out,
    frame_out,
    grad_queries,
    grad_event_values,
    grad_keys,
    grad_frame_values,
    far_a_t,
    kept_scores,
    kept_terms,
    g_t,
    columns,
    ready,
    todo,
    sems,
):
    grad_a[...] = grad_a_in[...]
    grad_v[...] = grad_v_in[...]
    other_grads(near2, g_t, columns)
    count = pair_list(todo, plan[1], read_code(near1, 0))
    known = near1, near2, near_a_t, g_t, columns, self_a, self_v, self_g, stats, grad_a, grad_v, todo
    back(*known, 0, jnp.minimum(count, HELD), near_scores)
    back(*known, HELD, count)
    outs = (grad_queries, grad_event_values, grad_keys, grad_frame_values)
    code = read_code(far1, 1)
    later = touched_blocks(plan[2], code)
    copies = []
    for me in range(4):

        @pl.when(jnp.logical_not(later[me]))
        def _():
            send_grads(me, grad_a, grad_v, ready, outs, sems)

    for me in range(4):
        low = (me % 2) * BLOCK
        ready[8 + me] = normed_t[me].T
        copies += start_all(
            (ready.at[8 + me], (event_out, frame_out)[me // 2].at[low : low + BLOCK], sems.at[8 + me])
        )
    other_queries(far1, far_a_t)
    count = pair_list(todo, plan[2], code)
    part_way(far1, self_a, self_g, stats, kept_scores, kept_terms, todo, jnp.minimum(count, KEPT))
    for c in copies:
        c.wait()
    for me in range(4):

        @pl.when(jnp.logical_not(later[me]))
        def _():
            wait_grads(me, ready, outs, sems)


def far_backward(
    plan,
    far1,
    far2,
    self_a,
    self_v,
    self_g,
    far_a_t,
    stats,
    kept_scores,
    kept_terms,
    grad_a_in,
    grad_v_in,
    _queries,
    _event_values,
    _keys,
    _frame_values,
    grad_queries,
    grad_event_values,
    grad_keys,
    grad_frame_values,
    grad_a,
    grad_v,
    g_t,
    columns,
    ready,
    todo,
    sems,
):
    code = read_code(far1, 1)
    touched = touched_blocks(plan[2], code)
    outs = (grad_queries, grad_event_values, grad_keys, grad_frame_values)
    count = pair_list(todo, plan[2], code)

    @pl.when(count > 0)
    def _():
        for me in range(4):

            @pl.when(touched[me])
            def _():
                grad_a[me] = grad_a_in[me]
                grad_v[me] = grad_v_in[me]

        other_grads(far2, g_t, columns)
        begun = jnp.minimum(count, KEPT)
        back_rest(far2, far_a_t, g_t, columns, self_v, kept_scores, kept_terms, grad_a, grad_v, todo, begun)
        back(
            far1, far2, far_a_t, g_t, columns, self_a, self_v, self_g, stats, grad_a, grad_v, todo, begun, count
        )
        for me in range(4):

            @pl.when(touched[me])
            def _():
                send_grads(me, grad_a, grad_v, ready, outs, sems)

        for me in range(4):

            @pl.when(touched[me])
            def _():
                wait_grads(me, ready, outs, sems)


def shape(*dims, dtype=F32):
    return jax.ShapeDtypeStruct(dims, dtype)


def specs(kinds):
    space = {"s": pltpu.SMEM, "v": pltpu.VMEM, "h": pltpu.HBM}
    return [pl.BlockSpec(memory_space=space[k]) for k in kinds]


def kernel(body, operands, places, outs, out_places, scratch=(), flops=0, limit=VMEM_LIMIT, aliases=()):
    return pl.pallas_call(
        body,
        out_shape=tuple(outs),
        in_specs=specs(places),
        out_specs=tuple(specs(out_places)),
        scratch_shapes=list(scratch),
        compiler_params=params(limit),
        cost_estimate=cost(flops),
        input_output_aliases=dict(aliases),
    )(*operands)


def on_device(
    event_queries,
    event_values,
    frame_keys,
    frame_values,
    partner,
    live_count,
    event_cotangent,
    frame_cotangent,
):
    width = FEATS * lax.axis_size("hd")
    runs = lax.axis_size("st")
    inner_pairs = [(i, i ^ 1) for i in range(runs)]
    outer_pairs = [(i, i + 1) for i in range(1, runs - 1, 2)] + [(i + 1, i) for i in range(1, runs - 1, 2)]
    tile = (4, FEATS, BLOCK)
    wide = (4, HEADS, PAIR, BLOCK)
    small = (4, 2 * HEADS, BLOCK)
    todo = pltpu.SMEM((16,), jnp.int32)

    far_msg1, plan = kernel(
        pack_kernel,
        (partner, live_count, event_queries, event_values, frame_keys, frame_values),
        "hhhhhh",
        (shape(FAR1, FEATS, dtype=BF16), shape(8, dtype=jnp.int32)),
        "vs",
        [
            pltpu.SMEM((2, SLOTS), jnp.int32),
            pltpu.SMEM((2,), jnp.int32),
            pltpu.SemaphoreType.DMA((6,)),
        ],
        limit=PACK_LIMIT,
    )
    far1 = lax.ppermute(far_msg1, "st", outer_pairs)
    msg1 = far_msg1[0:MSG1]
    near1 = lax.ppermute(msg1, "st", inner_pairs)

    held = shape(HELD + 1, HEADS, BLOCK, BLOCK)
    self_a, self_v, cot_t, soft, acc, near_a_t, own_scores, near_scores = kernel(
        near_forward,
        (plan, msg1, near1, event_cotangent, frame_cotangent),
        "svvhh",
        (
            shape(*wide, dtype=BF16),
            shape(*wide, dtype=BF16),
            shape(*tile, dtype=BF16),
            shape(*small),
            shape(*tile),
            shape(*tile, dtype=BF16),
            held,
            held,
        ),
        "vvvvvvvv",
        [
            pltpu.VMEM((2, ROWS, FEATS), BF16),
            pltpu.VMEM(tile, BF16),
            pltpu.VMEM(tile, BF16),
            todo,
            pltpu.SemaphoreType.DMA((2,)),
        ],
        1e6,
    )
    att, lse, sums = kernel(
        far_forward,
        (plan, far1, self_a, cot_t, soft, acc),
        "svvvvv",
        (shape(*tile), shape(*small), shape(lax.axis_size("hd"), 8, BLOCK)),
        "vvv",
        [
            pltpu.VMEM(small, F32),
            pltpu.VMEM(tile, BF16),
            pltpu.VMEM((1, HEADS, BLOCK, BLOCK), F32),
            todo,
        ],
        1e6,
    )
    sums = lax.all_to_all(sums, "hd", 0, 0)

    grad_t, normed_t, stats, msg2, far_msg2 = kernel(
        lambda *refs: grad_kernel(width, *refs),
        (att, cot_t, lse, sums),
        "vvvv",
        (
            shape(*tile, dtype=BF16),
            shape(*tile, dtype=BF16),
            shape(*small),
            shape(MSG2, FEATS, dtype=BF16),
            shape(FAR2, FEATS, dtype=BF16),
        ),
        "vvvvv",
        flops=1e6,
    )
    far2 = lax.ppermute(far_msg2, "st", outer_pairs)
    near2 = lax.ppermute(msg2, "st", inner_pairs)

    self_g, grad_a, grad_v = kernel(
        own_backward,
        (plan, msg1, msg2, self_a, self_v, grad_t, stats, own_scores),
        "svvvvvvv",
        (shape(*wide, dtype=BF16), shape(*tile), shape(*tile)),
        "vvv",
        [pltpu.VMEM((2, BLOCK, PAIR), F32), todo],
        1e6,
    )
    whole = [shape(ROWS, FEATS, dtype=BF16)]
    grad_a, grad_v, event_out, frame_out, *grads, far_a_t, kept_scores, kept_terms = kernel(
        near_backward,
        (plan, near1, far1, near2, self_a, self_v, self_g, near_a_t, normed_t, stats, near_scores, grad_a, grad_v),
        "svvvvvvvvvvvv",
        [shape(*tile)] * 2 + whole * 6 + [shape(*tile, dtype=BF16)] + [shape(KEPT, HEADS, BLOCK, BLOCK)] * 2,
        "vvhhhhhhvvv",
        [
            pltpu.VMEM(tile, BF16),
            pltpu.VMEM((4, BLOCK, PAIR), F32),
            pltpu.VMEM((12, BLOCK, FEATS), BF16),
            todo,
            pltpu.SemaphoreType.DMA((12,)),
        ],
        1e6,
    )
    grads = kernel(
        far_backward,
        (plan, far1, far2, self_a, self_v, self_g, far_a_t, stats, kept_scores, kept_terms, grad_a, grad_v, *grads),
        "svvvvvvvvvvvhhhh",
        whole * 4,
        "hhhh",
        [
            pltpu.VMEM(tile, F32),
            pltpu.VMEM(tile, F32),
            pltpu.VMEM(tile, BF16),
            pltpu.VMEM((4, BLOCK, PAIR), F32),
            pltpu.VMEM((8, BLOCK, FEATS), BF16),
            todo,
            pltpu.SemaphoreType.DMA((8,)),
        ],
        1e6,
        aliases=((12, 0), (13, 1), (14, 2), (15, 3)),
    )
    return (event_out, frame_out) + tuple(grads)


def solution(mesh):
    tokens = P("st", "hd")
    return jax.shard_map(
        on_device,
        mesh=mesh,
        in_specs=(tokens, tokens, tokens, tokens, P("st", None), P("st"), tokens, tokens),
        out_specs=(tokens,) * 6,
        check_vma=False,
    )
```

```python
import jax
import jax.numpy as jnp
from jax import lax
from jax.experimental import pallas as pl
from jax.experimental.pallas import tpu as pltpu
from jax.sharding import PartitionSpec as P

DH = 64
BLOCK = 256
SLOTS = 3
HEADS = 4
FEATS = HEADS * DH
ROWS = 2 * BLOCK
PAIR = 2 * DH
EPS = 1e-06
NEG = -1e30
LOG2E = 1.4426950408889634
SCALE = DH**-0.5

KEYS, FVALS, QUERIES, EVALS, CODES = 0, ROWS, 2 * ROWS, 3 * ROWS, 4 * ROWS
MSG1 = 4 * ROWS + 16
FAR1 = MSG1 + 16
STATS = 2 * ROWS
MIDDLE = STATS + 4 * 8
LOW = MIDDLE + 4 * 8
MSG2 = LOW + 4 * 4
FAR2 = MSG2 + 16
KEPT = 3
HELD = 4

F32 = jnp.float32
BF16 = jnp.bfloat16
VMEM_LIMIT = 28 * 1024 * 1024
PACK_LIMIT = 62 * 1024 * 1024


def dot(a, b):
    return jnp.dot(a, b, preferred_element_type=F32)


def dot_other_way(a, b):
    return lax.dot_general(a, b, (((1,), (1,)), ((), ())), preferred_element_type=F32)


def params(limit=VMEM_LIMIT, **more):
    return pltpu.CompilerParams(vmem_limit_bytes=limit, **more)


def cost(flops):
    return pl.CostEstimate(flops=int(flops), bytes_accessed=1 << 10, transcendentals=0)


def lanes(head):
    return slice((head // 2) * PAIR, (head // 2 + 1) * PAIR)


def feats(head):
    return slice(head * DH, (head + 1) * DH)


def stacked(parts):
    return jnp.concatenate(parts, axis=0)


def start_all(*copies):
    made = [pltpu.make_async_copy(*c) for c in copies]
    for c in made:
        c.start()
    return made


def code_for(partner, live, run):
    code = jnp.int32(0)
    for a in range(2):
        for s in range(SLOTS):
            block = partner[a, s] - 2 * run
            hit = (s < live[a]) & (block >= 0) & (block < 2)
            code += jnp.where(hit, jnp.left_shift(1, 2 * a + jnp.clip(block, 0, 1)), 0)
    return code


def bits(code):
    return [
        (a, f, jnp.bitwise_and(jnp.right_shift(code, 2 * a + f), 1)) for a in range(2) for f in range(2)
    ]


def pair_list(todo, as_events, as_frames):
    count = jnp.int32(0)
    for a, f, hit in bits(as_events):
        todo[count] = a * 2 + f
        count += hit
    for a, f, hit in bits(as_frames):
        todo[count] = (2 + f) * 2 + a
        count += hit
    return count


def read_code(msg, half):
    part = msg[CODES:MSG1, half * PAIR : (half + 1) * PAIR].astype(F32)
    return jnp.max(part).astype(jnp.int32)


def masked(features_first, head):
    tile = features_first[lanes(head), :]
    row = lax.broadcasted_iota(jnp.int32, tile.shape, 0)
    return jnp.where(row // DH == head % 2, tile, jnp.zeros_like(tile))


def pack_kernel(partner_in, live_in, queries, event_values, keys, frame_values, msg, plan, partner, live, sems):
    parts = ((keys, KEYS), (frame_values, FVALS), (queries, QUERIES), (event_values, EVALS))
    tables = start_all((partner_in, partner, sems.at[0]), (live_in, live, sems.at[1]))
    arrays = start_all(*((part, msg.at[low : low + ROWS], sems.at[2 + i]) for i, (part, low) in enumerate(parts)))
    for c in tables:
        c.wait()
    run = lax.axis_index("st")
    odd = lax.rem(run, 2)
    plan[0] = code_for(partner, live, run)
    for half, target in enumerate((run + 1 - 2 * odd, run - 1 + 2 * odd)):
        code = code_for(partner, live, target)
        plan[1 + half] = code
        msg[CODES:FAR1, half * PAIR : (half + 1) * PAIR] = jnp.full((32, PAIR), code.astype(F32), F32).astype(BF16)
    for c in arrays:
        c.wait()


def attend(msg, vals_t, self_a, soft, acc, ahead, todo, count):
    slots = ahead.shape[0]

    def place(n):
        entry = todo[n]
        me = lax.div(entry, 2)
        side = lax.div(me, 2)
        block = lax.rem(entry, 2)
        return me, side * 2 + block, pl.multiple_of(side * (2 * ROWS) + block * BLOCK, BLOCK)

    def scores_of(n):
        me, _, row = place(n)
        return [dot(msg[pl.ds(row, BLOCK), lanes(h)], self_a[me, h]) for h in range(HEADS)]

    def keep(n, scores):
        slot = jnp.minimum(n, slots - 1)
        for h in range(HEADS):
            ahead[slot, h] = scores[h]

    @pl.when(count > 0)
    def _():
        keep(0, scores_of(0))

    def add(n, last):
        me, at, _ = place(n)
        old, whole = soft[me], acc[me]
        slot = jnp.minimum(n, slots - 1)
        scores = [ahead[slot, h] for h in range(HEADS)]
        if not last:
            following = scores_of(n + 1)
        tops, totals, decays, weights = [], [], [], []
        for h in range(HEADS):
            top = jnp.maximum(old[h : h + 1], jnp.max(scores[h], axis=0, keepdims=True))
            decay = jnp.exp(old[h : h + 1] - top)
            expo = jnp.exp(scores[h] - top)
            tops.append(top)
            decays.append(decay)
            totals.append(old[HEADS + h : HEADS + h + 1] * decay + jnp.sum(expo, axis=0, keepdims=True))
            weights.append(expo.astype(BF16))
        acc[me] = stacked(
            [whole[feats(h)] * decays[h] + dot(vals_t[at, feats(h), :], weights[h]) for h in range(HEADS)]
        )
        soft[me] = stacked(tops + totals)
        if not last:
            keep(n + 1, following)

    def pair(n, _):
        add(n, False)
        return 0

    lax.fori_loop(0, count - 1, pair, 0)

    @pl.when(count > 0)
    def _():
        add(count - 1, True)


def other_values(msg, vals_t):
    for side, base in ((0, FVALS), (1, EVALS)):
        for block in range(2):
            low = base + block * BLOCK
            vals_t[side * 2 + block] = msg[low : low + BLOCK, :].T


def other_queries(msg, a_t):
    for side, base in ((0, KEYS), (1, QUERIES)):
        for block in range(2):
            low = base + block * BLOCK
            a_t[side * 2 + block] = msg[low : low + BLOCK, :].T * BF16(SCALE)


def near_forward(
    plan,
    own,
    near,
    event_cot,
    frame_cot,
    self_a,
    self_v,
    cot_t,
    soft,
    acc,
    near_a_t,
    own_scores,
    near_scores,
    cots,
    own_vals,
    near_vals,
    todo,
    sems,
):
    fetched = start_all((event_cot, cots.at[0], sems.at[0]), (frame_cot, cots.at[1], sems.at[1]))
    for side, (base_a, base_v) in enumerate(((QUERIES, EVALS), (KEYS, FVALS))):
        for block in range(2):
            me = side * 2 + block
            low = block * BLOCK
            a_t = own[base_a + low : base_a + low + BLOCK, :].T * BF16(SCALE)
            v_t = own[base_v + low : base_v + low + BLOCK, :].T
            own_vals[(1 - side) * 2 + block] = v_t
            for h in range(HEADS):
                self_a[me, h] = masked(a_t, h)
                self_v[me, h] = masked(v_t, h)
            soft[me, 0:HEADS, :] = jnp.full((HEADS, BLOCK), NEG, F32)
            soft[me, HEADS : 2 * HEADS, :] = jnp.zeros((HEADS, BLOCK), F32)
            acc[me] = jnp.zeros((FEATS, BLOCK), F32)
    count = pair_list(todo, plan[0], plan[0])
    attend(own, own_vals, self_a, soft, acc, own_scores, todo, count)
    other_values(near, near_vals)
    count = pair_list(todo, plan[1], read_code(near, 0))
    attend(near, near_vals, self_a, soft, acc, near_scores, todo, count)
    other_queries(near, near_a_t)
    for c in fetched:
        c.wait()
    for me in range(4):
        low = (me % 2) * BLOCK
        cot_t[me] = cots[me // 2, low : low + BLOCK, :].T


def far_forward(plan, far, self_a, cot_t, soft_in, acc_in, att, lse, sums, soft, vals_t, ahead, todo):
    acc = att
    soft[...] = soft_in[...]
    acc[...] = acc_in[...]
    other_values(far, vals_t)
    count = pair_list(todo, plan[2], read_code(far, 1))
    attend(far, vals_t, self_a, soft, acc, ahead, todo, count)
    for me in range(4):
        old, whole = soft[me], acc[me]
        total = old[HEADS : 2 * HEADS]
        lse[me] = stacked([old[0:HEADS] * LOG2E + jnp.log2(total), jnp.zeros((HEADS, BLOCK), F32)])
        inverse = 1.0 / total
        values = stacked([whole[feats(h)] * inverse[h : h + 1] for h in range(HEADS)])
        att[me] = values
        square = jnp.sum(values * values, axis=0, keepdims=True)
        slope = jnp.sum(values * cot_t[me].astype(F32), axis=0, keepdims=True)
        for to in range(sums.shape[0]):
            sums[to, 2 * me : 2 * me + 1, :] = square
            sums[to, 2 * me + 1 : 2 * me + 2, :] = slope


def split(value):
    high = value.astype(BF16).astype(F32)
    rest = value - high
    middle = rest.astype(BF16).astype(F32)
    return high, middle, rest - middle


def grad_kernel(width, att, cot_t, lse, sums, grad_t, normed_t, stats, msg, far):
    whole = jnp.sum(sums[...], axis=0)
    parts = {}
    for me in range(4):
        rms = lax.rsqrt(whole[2 * me : 2 * me + 1, :] / width + EPS)
        slope = rms * whole[2 * me + 1 : 2 * me + 2, :] / width
        values = att[me]
        normed = values * rms
        grad = (rms * (cot_t[me].astype(F32) - normed * slope)).astype(BF16)
        grad_t[me] = grad
        normed_t[me] = normed.astype(BF16)
        side, block = 1 - me // 2, me % 2
        low = side * ROWS + block * BLOCK
        turned = grad.T
        msg[low : low + BLOCK, :] = turned
        far[low : low + BLOCK, :] = turned
        product = grad.astype(F32) * values
        deltas = [jnp.sum(product[feats(h)], axis=0, keepdims=True) for h in range(HEADS)]
        mine = stacked([lse[me, 0:HEADS, :]] + deltas)
        stats[me] = mine
        parts[2 * side + block] = split(mine)
    rows = stacked(
        [parts[at][0] for at in range(4)]
        + [parts[at][1] for at in range(4)]
        + [parts[at][2][0:HEADS] for at in range(4)]
    ).astype(BF16)
    msg[STATS:MSG2, :] = rows
    far[STATS:MSG2, :] = rows
    far[MSG2:FAR2, :] = jnp.zeros((16, FEATS), BF16)


def as_columns(rows):
    return stacked([rows, jnp.zeros((PAIR - 2 * HEADS, BLOCK), F32)]).T


def other_grads(msg, g_t, columns):
    high = msg[STATS:MIDDLE, :].astype(F32) + msg[MIDDLE:LOW, :].astype(F32)
    rest = msg[LOW:MSG2, :].astype(F32)
    for at in range(4):
        g_t[at] = msg[at * BLOCK : (at + 1) * BLOCK, :].T
        whole = high[8 * at : 8 * at + 8]
        columns[at] = as_columns(stacked([whole[0:HEADS] + rest[4 * at : 4 * at + 4], whole[HEADS : 2 * HEADS]]))


def in_order(dots, weigh, outs):
    dots(0)
    dots(1)
    dots(2)
    weigh(0)
    dots(3)
    for h in range(HEADS):
        outs(h)
        if h + 1 < HEADS:
            weigh(h + 1)


def slopes(made, row_stats, columns, h):
    scores, self_change, other_change = made
    scores = scores * LOG2E
    self_p = jnp.exp2(scores - row_stats[h : h + 1])
    other_p = jnp.exp2(scores - columns[:, h : h + 1])
    g = HEADS + h
    slope = self_p * (self_change - row_stats[g : g + 1]) + other_p * (other_change - columns[:, g : g + 1])
    return slope.astype(BF16), self_p.astype(BF16), other_p.astype(BF16)


def back(
    msg1, msg2, a_t, g_t, columns, self_a, self_v, self_g, stats, grad_a, grad_v, todo, first, count, held=None
):
    def pair(n, _):
        entry = todo[n]
        me = lax.div(entry, 2)
        side = lax.div(me, 2)
        block = lax.rem(entry, 2)
        row_a = pl.multiple_of(side * (2 * ROWS) + block * BLOCK, BLOCK)
        row_v = pl.multiple_of(side * (2 * ROWS) + ROWS + block * BLOCK, BLOCK)
        row_g = pl.multiple_of(side * ROWS + block * BLOCK, BLOCK)
        at = side * 2 + block
        mine, theirs = stats[me], columns[at]
        made, ready, sums = {}, {}, {}

        def dots(h):
            made[h] = (
                dot(msg1[pl.ds(row_a, BLOCK), lanes(h)], self_a[me, h]) if held is None else held[n, h],
                dot(msg1[pl.ds(row_v, BLOCK), lanes(h)], self_g[me, h]),
                dot(msg2[pl.ds(row_g, BLOCK), lanes(h)], self_v[me, h]),
            )

        def weigh(h):
            ready[h] = slopes(made[h], mine, theirs, h)

        def outs(h):
            slope, _, other_p = ready[h]
            sums[h] = dot(a_t[at, feats(h), :], slope), dot(g_t[at, feats(h), :], other_p)

        in_order(dots, weigh, outs)
        grad_a[me] += stacked([sums[h][0] for h in range(HEADS)])
        grad_v[me] += stacked([sums[h][1] for h in range(HEADS)])
        return 0

    lax.fori_loop(first, count, pair, 0)


def part_way(msg1, self_a, self_g, stats, kept_scores, kept_terms, todo, count):
    def pair(n, _):
        entry = todo[n]
        me = lax.div(entry, 2)
        side = lax.div(me, 2)
        block = lax.rem(entry, 2)
        row_a = pl.multiple_of(side * (2 * ROWS) + block * BLOCK, BLOCK)
        row_v = pl.multiple_of(side * (2 * ROWS) + ROWS + block * BLOCK, BLOCK)
        mine = stats[me]
        scores = [dot(msg1[pl.ds(row_a, BLOCK), lanes(h)], self_a[me, h]) * LOG2E for h in range(HEADS)]
        changes = [dot(msg1[pl.ds(row_v, BLOCK), lanes(h)], self_g[me, h]) for h in range(HEADS)]
        for h in range(HEADS):
            g = HEADS + h
            kept_scores[n, h] = scores[h]
            kept_terms[n, h] = jnp.exp2(scores[h] - mine[h : h + 1]) * (changes[h] - mine[g : g + 1])
        return 0

    lax.fori_loop(0, count, pair, 0)


def back_rest(msg2, a_t, g_t, columns, self_v, kept_scores, kept_terms, grad_a, grad_v, todo, count):
    def pair(n, _):
        entry = todo[n]
        me = lax.div(entry, 2)
        side = lax.div(me, 2)
        block = lax.rem(entry, 2)
        row_g = pl.multiple_of(side * ROWS + block * BLOCK, BLOCK)
        at = side * 2 + block
        theirs = columns[at]
        made, ready, sums = {}, {}, {}

        def dots(h):
            made[h] = dot(msg2[pl.ds(row_g, BLOCK), lanes(h)], self_v[me, h])

        def weigh(h):
            g = HEADS + h
            other_p = jnp.exp2(kept_scores[n, h] - theirs[:, h : h + 1])
            slope = kept_terms[n, h] + other_p * (made[h] - theirs[:, g : g + 1])
            ready[h] = slope.astype(BF16), other_p.astype(BF16)

        def outs(h):
            slope, other_p = ready[h]
            sums[h] = dot(a_t[at, feats(h), :], slope), dot(g_t[at, feats(h), :], other_p)

        in_order(dots, weigh, outs)
        grad_a[me] += stacked([sums[h][0] for h in range(HEADS)])
        grad_v[me] += stacked([sums[h][1] for h in range(HEADS)])
        return 0

    lax.fori_loop(0, count, pair, 0)


def back_own(msg1, msg2, columns, self_a, self_v, self_g, grad_t, stats, held, grad_a, grad_v, todo, count):
    def pair(n, _):
        entry = todo[n]
        me = lax.div(entry, 2)
        block = lax.rem(entry, 2)
        frame = 2 + block
        row_v = pl.multiple_of(FVALS + block * BLOCK, BLOCK)
        row_g = pl.multiple_of(block * BLOCK, BLOCK)
        mine, theirs = stats[me], columns[block]
        made, ready, sums = {}, {}, {}

        def dots(h):
            made[h] = (
                held[n, h],
                dot(msg1[pl.ds(row_v, BLOCK), lanes(h)], self_g[me, h]),
                dot(msg2[pl.ds(row_g, BLOCK), lanes(h)], self_v[me, h]),
            )

        def weigh(h):
            ready[h] = slopes(made[h], mine, theirs, h)

        def outs(h):
            slope, self_p, other_p = ready[h]
            half = slice((h % 2) * DH, (h % 2 + 1) * DH)
            sums[h] = (
                dot(self_a[frame, h, half, :], slope),
                dot(grad_t[frame, feats(h), :], other_p),
                dot_other_way(self_a[me, h, half, :], slope),
                dot_other_way(grad_t[me, feats(h), :], self_p),
            )

        in_order(dots, weigh, outs)
        grad_a[me] += stacked([sums[h][0] for h in range(HEADS)])
        grad_v[me] += stacked([sums[h][1] for h in range(HEADS)])
        grad_a[frame] += stacked([sums[h][2] for h in range(HEADS)])
        grad_v[frame] += stacked([sums[h][3] for h in range(HEADS)])
        return 0

    lax.fori_loop(0, count, pair, 0)


def own_backward(
    plan, own1, own2, self_a, self_v, grad_t, stats, own_scores, self_g, grad_a, grad_v, columns, todo
):
    for me in range(4):
        for h in range(HEADS):
            self_g[me, h] = masked(grad_t[me], h)
        grad_a[me] = jnp.zeros((FEATS, BLOCK), F32)
        grad_v[me] = jnp.zeros((FEATS, BLOCK), F32)
    for block in range(2):
        columns[block] = as_columns(stats[2 + block])
    count = pair_list(todo, plan[0], jnp.int32(0))
    back_own(own1, own2, columns, self_a, self_v, self_g, grad_t, stats, own_scores, grad_a, grad_v, todo, count)


def touched_blocks(as_events, as_frames):
    return [jnp.bitwise_and(as_events, 3 * 4**a) != 0 for a in range(2)] + [
        jnp.bitwise_and(as_frames, 5 * 2**f) != 0 for f in range(2)
    ]


def wait_grads(me, ready, outs, sems):
    side, low = me // 2, (me % 2) * BLOCK
    for k in range(2):
        at = 2 * me + k
        pltpu.make_async_copy(ready.at[at], outs[2 * side + k].at[low : low + BLOCK], sems.at[at]).wait()


def send_grads(me, grad_a, grad_v, ready, outs, sems):
    side, low = me // 2, (me % 2) * BLOCK
    for k, grad in enumerate((grad_a, grad_v)):
        ready[2 * me + k] = grad[me].astype(BF16).T
        start_all((ready.at[2 * me + k], outs[2 * side + k].at[low : low + BLOCK], sems.at[2 * me + k]))


def near_backward(
    plan,
    near1,
    far1,
    near2,
    self_a,
    self_v,
    self_g,
    near_a_t,
    normed_t,
    stats,
    near_scores,
    grad_a_in,
    grad_v_in,
    grad_a,
    grad_v,
    event_out,
    frame_out,
    grad_queries,
    grad_event_values,
    grad_keys,
    grad_frame_values,
    far_a_t,
    kept_scores,
    kept_terms,
    g_t,
    columns,
    ready,
    todo,
    sems,
):
    grad_a[...] = grad_a_in[...]
    grad_v[...] = grad_v_in[...]
    other_grads(near2, g_t, columns)
    count = pair_list(todo, plan[1], read_code(near1, 0))
    known = near1, near2, near_a_t, g_t, columns, self_a, self_v, self_g, stats, grad_a, grad_v, todo
    back(*known, 0, jnp.minimum(count, HELD), near_scores)
    back(*known, HELD, count)
    outs = (grad_queries, grad_event_values, grad_keys, grad_frame_values)
    code = read_code(far1, 1)
    later = touched_blocks(plan[2], code)
    copies = []
    for me in range(4):

        @pl.when(jnp.logical_not(later[me]))
        def _():
            send_grads(me, grad_a, grad_v, ready, outs, sems)

    for me in range(4):
        low = (me % 2) * BLOCK
        ready[8 + me] = normed_t[me].T
        copies += start_all(
            (ready.at[8 + me], (event_out, frame_out)[me // 2].at[low : low + BLOCK], sems.at[8 + me])
        )
    other_queries(far1, far_a_t)
    count = pair_list(todo, plan[2], code)
    part_way(far1, self_a, self_g, stats, kept_scores, kept_terms, todo, jnp.minimum(count, KEPT))
    for c in copies:
        c.wait()
    for me in range(4):

        @pl.when(jnp.logical_not(later[me]))
        def _():
            wait_grads(me, ready, outs, sems)


def far_backward(
    plan,
    far1,
    far2,
    self_a,
    self_v,
    self_g,
    far_a_t,
    stats,
    kept_scores,
    kept_terms,
    grad_a_in,
    grad_v_in,
    _queries,
    _event_values,
    _keys,
    _frame_values,
    grad_queries,
    grad_event_values,
    grad_keys,
    grad_frame_values,
    grad_a,
    grad_v,
    g_t,
    columns,
    ready,
    todo,
    sems,
):
    code = read_code(far1, 1)
    touched = touched_blocks(plan[2], code)
    outs = (grad_queries, grad_event_values, grad_keys, grad_frame_values)
    count = pair_list(todo, plan[2], code)

    @pl.when(count > 0)
    def _():
        for me in range(4):

            @pl.when(touched[me])
            def _():
                grad_a[me] = grad_a_in[me]
                grad_v[me] = grad_v_in[me]

        other_grads(far2, g_t, columns)
        begun = jnp.minimum(count, KEPT)
        back_rest(far2, far_a_t, g_t, columns, self_v, kept_scores, kept_terms, grad_a, grad_v, todo, begun)
        back(
            far1, far2, far_a_t, g_t, columns, self_a, self_v, self_g, stats, grad_a, grad_v, todo, begun, count
        )
        for me in range(4):

            @pl.when(touched[me])
            def _():
                send_grads(me, grad_a, grad_v, ready, outs, sems)

        for me in range(4):

            @pl.when(touched[me])
            def _():
                wait_grads(me, ready, outs, sems)


def shape(*dims, dtype=F32):
    return jax.ShapeDtypeStruct(dims, dtype)


def specs(kinds):
    space = {"s": pltpu.SMEM, "v": pltpu.VMEM, "h": pltpu.HBM}
    return [pl.BlockSpec(memory_space=space[k]) for k in kinds]


def kernel(body, operands, places, outs, out_places, scratch=(), flops=0, limit=VMEM_LIMIT, aliases=()):
    return pl.pallas_call(
        body,
        out_shape=tuple(outs),
        in_specs=specs(places),
        out_specs=tuple(specs(out_places)),
        scratch_shapes=list(scratch),
        compiler_params=params(limit),
        cost_estimate=cost(flops),
        input_output_aliases=dict(aliases),
    )(*operands)


def on_device(
    event_queries,
    event_values,
    frame_keys,
    frame_values,
    partner,
    live_count,
    event_cotangent,
    frame_cotangent,
):
    width = FEATS * lax.axis_size("hd")
    runs = lax.axis_size("st")
    inner_pairs = [(i, i ^ 1) for i in range(runs)]
    outer_pairs = [(i, i + 1) for i in range(1, runs - 1, 2)] + [(i + 1, i) for i in range(1, runs - 1, 2)]
    tile = (4, FEATS, BLOCK)
    wide = (4, HEADS, PAIR, BLOCK)
    small = (4, 2 * HEADS, BLOCK)
    todo = pltpu.SMEM((16,), jnp.int32)

    far_msg1, plan = kernel(
        pack_kernel,
        (partner, live_count, event_queries, event_values, frame_keys, frame_values),
        "hhhhhh",
        (shape(FAR1, FEATS, dtype=BF16), shape(8, dtype=jnp.int32)),
        "vs",
        [
            pltpu.SMEM((2, SLOTS), jnp.int32),
            pltpu.SMEM((2,), jnp.int32),
            pltpu.SemaphoreType.DMA((6,)),
        ],
        limit=PACK_LIMIT,
    )
    far1 = lax.ppermute(far_msg1, "st", outer_pairs)
    msg1 = far_msg1[0:MSG1]
    near1 = lax.ppermute(msg1, "st", inner_pairs)

    held = shape(HELD + 1, HEADS, BLOCK, BLOCK)
    self_a, self_v, cot_t, soft, acc, near_a_t, own_scores, near_scores = kernel(
        near_forward,
        (plan, msg1, near1, event_cotangent, frame_cotangent),
        "svvhh",
        (
            shape(*wide, dtype=BF16),
            shape(*wide, dtype=BF16),
            shape(*tile, dtype=BF16),
            shape(*small),
            shape(*tile),
            shape(*tile, dtype=BF16),
            held,
            held,
        ),
        "vvvvvvvv",
        [
            pltpu.VMEM((2, ROWS, FEATS), BF16),
            pltpu.VMEM(tile, BF16),
            pltpu.VMEM(tile, BF16),
            todo,
            pltpu.SemaphoreType.DMA((2,)),
        ],
        1e6,
    )
    att, lse, sums = kernel(
        far_forward,
        (plan, far1, self_a, cot_t, soft, acc),
        "svvvvv",
        (shape(*tile), shape(*small), shape(lax.axis_size("hd"), 8, BLOCK)),
        "vvv",
        [
            pltpu.VMEM(small, F32),
            pltpu.VMEM(tile, BF16),
            pltpu.VMEM((1, HEADS, BLOCK, BLOCK), F32),
            todo,
        ],
        1e6,
    )
    sums = lax.all_to_all(sums, "hd", 0, 0)

    grad_t, normed_t, stats, msg2, far_msg2 = kernel(
        lambda *refs: grad_kernel(width, *refs),
        (att, cot_t, lse, sums),
        "vvvv",
        (
            shape(*tile, dtype=BF16),
            shape(*tile, dtype=BF16),
            shape(*small),
            shape(MSG2, FEATS, dtype=BF16),
            shape(FAR2, FEATS, dtype=BF16),
        ),
        "vvvvv",
        flops=1e6,
    )
    far2 = lax.ppermute(far_msg2, "st", outer_pairs)
    near2 = lax.ppermute(msg2, "st", inner_pairs)

    self_g, grad_a, grad_v = kernel(
        own_backward,
        (plan, msg1, msg2, self_a, self_v, grad_t, stats, own_scores),
        "svvvvvvv",
        (shape(*wide, dtype=BF16), shape(*tile), shape(*tile)),
        "vvv",
        [pltpu.VMEM((2, BLOCK, PAIR), F32), todo],
        1e6,
    )
    whole = [shape(ROWS, FEATS, dtype=BF16)]
    grad_a, grad_v, event_out, frame_out, *grads, far_a_t, kept_scores, kept_terms = kernel(
        near_backward,
        (plan, near1, far1, near2, self_a, self_v, self_g, near_a_t, normed_t, stats, near_scores, grad_a, grad_v),
        "svvvvvvvvvvvv",
        [shape(*tile)] * 2 + whole * 6 + [shape(*tile, dtype=BF16)] + [shape(KEPT, HEADS, BLOCK, BLOCK)] * 2,
        "vvhhhhhhvvv",
        [
            pltpu.VMEM(tile, BF16),
            pltpu.VMEM((4, BLOCK, PAIR), F32),
            pltpu.VMEM((12, BLOCK, FEATS), BF16),
            todo,
            pltpu.SemaphoreType.DMA((12,)),
        ],
        1e6,
    )
    grads = kernel(
        far_backward,
        (plan, far1, far2, self_a, self_v, self_g, far_a_t, stats, kept_scores, kept_terms, grad_a, grad_v, *grads),
        "svvvvvvvvvvvhhhh",
        whole * 4,
        "hhhh",
        [
            pltpu.VMEM(tile, F32),
            pltpu.VMEM(tile, F32),
            pltpu.VMEM(tile, BF16),
            pltpu.VMEM((4, BLOCK, PAIR), F32),
            pltpu.VMEM((8, BLOCK, FEATS), BF16),
            todo,
            pltpu.SemaphoreType.DMA((8,)),
        ],
        1e6,
        aliases=((12, 0), (13, 1), (14, 2), (15, 3)),
    )
    return (event_out, frame_out) + tuple(grads)


def solution(mesh):
    tokens = P("st", "hd")
    return jax.shard_map(
        on_device,
        mesh=mesh,
        in_specs=(tokens, tokens, tokens, tokens, P("st", None), P("st"), tokens, tokens),
        out_specs=(tokens,) * 6,
        check_vma=False,
    )
```

```python
import jax
import jax.numpy as jnp
from jax import lax
from jax.experimental import pallas as pl
from jax.experimental.pallas import tpu as pltpu
from jax.sharding import PartitionSpec as P

DH = 64
BLOCK = 256
SLOTS = 3
HEADS = 4
FEATS = HEADS * DH
ROWS = 2 * BLOCK
PAIR = 2 * DH
EPS = 1e-06
NEG = -1e30
LOG2E = 1.4426950408889634
SCALE = DH**-0.5

KEYS, FVALS, QUERIES, EVALS, CODES = 0, ROWS, 2 * ROWS, 3 * ROWS, 4 * ROWS
MSG1 = 4 * ROWS + 16
FAR1 = MSG1 + 16
STATS = 2 * ROWS
MIDDLE = STATS + 4 * 8
LOW = MIDDLE + 4 * 8
MSG2 = LOW + 4 * 4
FAR2 = MSG2 + 16
KEPT = 1
HELD = 4

F32 = jnp.float32
BF16 = jnp.bfloat16
VMEM_LIMIT = 28 * 1024 * 1024
PACK_LIMIT = 62 * 1024 * 1024


def dot(a, b):
    return jnp.dot(a, b, preferred_element_type=F32)


def dot_other_way(a, b):
    return lax.dot_general(a, b, (((1,), (1,)), ((), ())), preferred_element_type=F32)


def params(limit=VMEM_LIMIT, **more):
    return pltpu.CompilerParams(vmem_limit_bytes=limit, **more)


def cost(flops):
    return pl.CostEstimate(flops=int(flops), bytes_accessed=1 << 10, transcendentals=0)


def lanes(head):
    return slice((head // 2) * PAIR, (head // 2 + 1) * PAIR)


def feats(head):
    return slice(head * DH, (head + 1) * DH)


def stacked(parts):
    return jnp.concatenate(parts, axis=0)


def start_all(*copies):
    made = [pltpu.make_async_copy(*c) for c in copies]
    for c in made:
        c.start()
    return made


def code_for(partner, live, run):
    code = jnp.int32(0)
    for a in range(2):
        for s in range(SLOTS):
            block = partner[a, s] - 2 * run
            hit = (s < live[a]) & (block >= 0) & (block < 2)
            code += jnp.where(hit, jnp.left_shift(1, 2 * a + jnp.clip(block, 0, 1)), 0)
    return code


def bits(code):
    return [
        (a, f, jnp.bitwise_and(jnp.right_shift(code, 2 * a + f), 1)) for a in range(2) for f in range(2)
    ]


def pair_list(todo, as_events, as_frames):
    count = jnp.int32(0)
    for a, f, hit in bits(as_events):
        todo[count] = a * 2 + f
        count += hit
    for a, f, hit in bits(as_frames):
        todo[count] = (2 + f) * 2 + a
        count += hit
    return count


def read_code(msg, half):
    part = msg[CODES:MSG1, half * PAIR : (half + 1) * PAIR].astype(F32)
    return jnp.max(part).astype(jnp.int32)


def masked(features_first, head):
    tile = features_first[lanes(head), :]
    row = lax.broadcasted_iota(jnp.int32, tile.shape, 0)
    return jnp.where(row // DH == head % 2, tile, jnp.zeros_like(tile))


def pack_kernel(partner_in, live_in, queries, event_values, keys, frame_values, msg, plan, partner, live, sems):
    parts = ((keys, KEYS), (frame_values, FVALS), (queries, QUERIES), (event_values, EVALS))
    tables = start_all((partner_in, partner, sems.at[0]), (live_in, live, sems.at[1]))
    arrays = start_all(*((part, msg.at[low : low + ROWS], sems.at[2 + i]) for i, (part, low) in enumerate(parts)))
    for c in tables:
        c.wait()
    run = lax.axis_index("st")
    odd = lax.rem(run, 2)
    plan[0] = code_for(partner, live, run)
    for half, target in enumerate((run + 1 - 2 * odd, run - 1 + 2 * odd)):
        code = code_for(partner, live, target)
        plan[1 + half] = code
        msg[CODES:FAR1, half * PAIR : (half + 1) * PAIR] = jnp.full((32, PAIR), code.astype(F32), F32).astype(BF16)
    for c in arrays:
        c.wait()


def attend(msg, vals_t, self_a, soft, acc, ahead, todo, count):
    slots = ahead.shape[0]

    def place(n):
        entry = todo[n]
        me = lax.div(entry, 2)
        side = lax.div(me, 2)
        block = lax.rem(entry, 2)
        return me, side * 2 + block, pl.multiple_of(side * (2 * ROWS) + block * BLOCK, BLOCK)

    def scores_of(n):
        me, _, row = place(n)
        return [dot(msg[pl.ds(row, BLOCK), lanes(h)], self_a[me, h]) for h in range(HEADS)]

    def keep(n, scores):
        slot = jnp.minimum(n, slots - 1)
        for h in range(HEADS):
            ahead[slot, h] = scores[h]

    keep(0, scores_of(0))

    def pair(n, _):
        me, at, _ = place(n)
        old, whole = soft[me], acc[me]
        slot = jnp.minimum(n, slots - 1)
        scores = [ahead[slot, h] for h in range(HEADS)]
        after = jnp.minimum(n + 1, count - 1)
        following = scores_of(after)
        tops, totals, decays, weights = [], [], [], []
        for h in range(HEADS):
            top = jnp.maximum(old[h : h + 1], jnp.max(scores[h], axis=0, keepdims=True))
            decay = jnp.exp(old[h : h + 1] - top)
            expo = jnp.exp(scores[h] - top)
            tops.append(top)
            decays.append(decay)
            totals.append(old[HEADS + h : HEADS + h + 1] * decay + jnp.sum(expo, axis=0, keepdims=True))
            weights.append(expo.astype(BF16))
        acc[me] = stacked(
            [whole[feats(h)] * decays[h] + dot(vals_t[at, feats(h), :], weights[h]) for h in range(HEADS)]
        )
        soft[me] = stacked(tops + totals)
        keep(after, following)
        return 0

    lax.fori_loop(0, count, pair, 0)


def other_values(msg, vals_t):
    for side, base in ((0, FVALS), (1, EVALS)):
        for block in range(2):
            low = base + block * BLOCK
            vals_t[side * 2 + block] = msg[low : low + BLOCK, :].T


def other_queries(msg, a_t):
    for side, base in ((0, KEYS), (1, QUERIES)):
        for block in range(2):
            low = base + block * BLOCK
            a_t[side * 2 + block] = msg[low : low + BLOCK, :].T * BF16(SCALE)


def near_forward(
    plan,
    own,
    near,
    event_cot,
    frame_cot,
    self_a,
    self_v,
    cot_t,
    soft,
    acc,
    near_a_t,
    own_scores,
    near_scores,
    cots,
    own_vals,
    near_vals,
    todo,
    sems,
):
    fetched = start_all((event_cot, cots.at[0], sems.at[0]), (frame_cot, cots.at[1], sems.at[1]))
    for side, (base_a, base_v) in enumerate(((QUERIES, EVALS), (KEYS, FVALS))):
        for block in range(2):
            me = side * 2 + block
            low = block * BLOCK
            a_t = own[base_a + low : base_a + low + BLOCK, :].T * BF16(SCALE)
            v_t = own[base_v + low : base_v + low + BLOCK, :].T
            own_vals[(1 - side) * 2 + block] = v_t
            for h in range(HEADS):
                self_a[me, h] = masked(a_t, h)
                self_v[me, h] = masked(v_t, h)
            soft[me, 0:HEADS, :] = jnp.full((HEADS, BLOCK), NEG, F32)
            soft[me, HEADS : 2 * HEADS, :] = jnp.zeros((HEADS, BLOCK), F32)
            acc[me] = jnp.zeros((FEATS, BLOCK), F32)
    count = pair_list(todo, plan[0], plan[0])
    attend(own, own_vals, self_a, soft, acc, own_scores, todo, count)
    other_values(near, near_vals)
    count = pair_list(todo, plan[1], read_code(near, 0))
    attend(near, near_vals, self_a, soft, acc, near_scores, todo, count)
    other_queries(near, near_a_t)
    for c in fetched:
        c.wait()
    for me in range(4):
        low = (me % 2) * BLOCK
        cot_t[me] = cots[me // 2, low : low + BLOCK, :].T


def far_forward(plan, far, self_a, cot_t, soft_in, acc_in, att, lse, sums, soft, vals_t, ahead, todo):
    acc = att
    soft[...] = soft_in[...]
    acc[...] = acc_in[...]
    other_values(far, vals_t)
    count = pair_list(todo, plan[2], read_code(far, 1))
    attend(far, vals_t, self_a, soft, acc, ahead, todo, count)
    for me in range(4):
        old, whole = soft[me], acc[me]
        total = old[HEADS : 2 * HEADS]
        lse[me] = stacked([old[0:HEADS] * LOG2E + jnp.log2(total), jnp.zeros((HEADS, BLOCK), F32)])
        inverse = 1.0 / total
        values = stacked([whole[feats(h)] * inverse[h : h + 1] for h in range(HEADS)])
        att[me] = values
        square = jnp.sum(values * values, axis=0, keepdims=True)
        slope = jnp.sum(values * cot_t[me].astype(F32), axis=0, keepdims=True)
        for to in range(sums.shape[0]):
            sums[to, 2 * me : 2 * me + 1, :] = square
            sums[to, 2 * me + 1 : 2 * me + 2, :] = slope


def split(value):
    high = value.astype(BF16).astype(F32)
    rest = value - high
    middle = rest.astype(BF16).astype(F32)
    return high, middle, rest - middle


def grad_kernel(width, att, cot_t, lse, sums, grad_t, normed_t, stats, msg, far):
    whole = jnp.sum(sums[...], axis=0)
    parts = {}
    for me in range(4):
        rms = lax.rsqrt(whole[2 * me : 2 * me + 1, :] / width + EPS)
        slope = rms * whole[2 * me + 1 : 2 * me + 2, :] / width
        values = att[me]
        normed = values * rms
        grad = (rms * (cot_t[me].astype(F32) - normed * slope)).astype(BF16)
        grad_t[me] = grad
        normed_t[me] = normed.astype(BF16)
        side, block = 1 - me // 2, me % 2
        low = side * ROWS + block * BLOCK
        turned = grad.T
        msg[low : low + BLOCK, :] = turned
        far[low : low + BLOCK, :] = turned
        product = grad.astype(F32) * values
        deltas = [jnp.sum(product[feats(h)], axis=0, keepdims=True) for h in range(HEADS)]
        mine = stacked([lse[me, 0:HEADS, :]] + deltas)
        stats[me] = mine
        parts[2 * side + block] = split(mine)
    rows = stacked(
        [parts[at][0] for at in range(4)]
        + [parts[at][1] for at in range(4)]
        + [parts[at][2][0:HEADS] for at in range(4)]
    ).astype(BF16)
    msg[STATS:MSG2, :] = rows
    far[STATS:MSG2, :] = rows
    far[MSG2:FAR2, :] = jnp.zeros((16, FEATS), BF16)


def as_columns(rows):
    return stacked([rows, jnp.zeros((PAIR - 2 * HEADS, BLOCK), F32)]).T


def other_grads(msg, g_t, columns):
    high = msg[STATS:MIDDLE, :].astype(F32) + msg[MIDDLE:LOW, :].astype(F32)
    rest = msg[LOW:MSG2, :].astype(F32)
    for at in range(4):
        g_t[at] = msg[at * BLOCK : (at + 1) * BLOCK, :].T
        whole = high[8 * at : 8 * at + 8]
        columns[at] = as_columns(stacked([whole[0:HEADS] + rest[4 * at : 4 * at + 4], whole[HEADS : 2 * HEADS]]))


def in_order(dots, weigh, outs):
    dots(0)
    dots(1)
    dots(2)
    weigh(0)
    dots(3)
    for h in range(HEADS):
        outs(h)
        if h + 1 < HEADS:
            weigh(h + 1)


def slopes(made, row_stats, columns, h):
    scores, self_change, other_change = made
    scores = scores * LOG2E
    self_p = jnp.exp2(scores - row_stats[h : h + 1])
    other_p = jnp.exp2(scores - columns[:, h : h + 1])
    g = HEADS + h
    slope = self_p * (self_change - row_stats[g : g + 1]) + other_p * (other_change - columns[:, g : g + 1])
    return slope.astype(BF16), self_p.astype(BF16), other_p.astype(BF16)


def back(
    msg1, msg2, a_t, g_t, columns, self_a, self_v, self_g, stats, grad_a, grad_v, todo, first, count, held=None
):
    def pair(n, _):
        entry = todo[n]
        me = lax.div(entry, 2)
        side = lax.div(me, 2)
        block = lax.rem(entry, 2)
        row_a = pl.multiple_of(side * (2 * ROWS) + block * BLOCK, BLOCK)
        row_v = pl.multiple_of(side * (2 * ROWS) + ROWS + block * BLOCK, BLOCK)
        row_g = pl.multiple_of(side * ROWS + block * BLOCK, BLOCK)
        at = side * 2 + block
        mine, theirs = stats[me], columns[at]
        made, ready, sums = {}, {}, {}

        def dots(h):
            made[h] = (
                dot(msg1[pl.ds(row_a, BLOCK), lanes(h)], self_a[me, h]) if held is None else held[n, h],
                dot(msg1[pl.ds(row_v, BLOCK), lanes(h)], self_g[me, h]),
                dot(msg2[pl.ds(row_g, BLOCK), lanes(h)], self_v[me, h]),
            )

        def weigh(h):
            ready[h] = slopes(made[h], mine, theirs, h)

        def outs(h):
            slope, _, other_p = ready[h]
            sums[h] = dot(a_t[at, feats(h), :], slope), dot(g_t[at, feats(h), :], other_p)

        in_order(dots, weigh, outs)
        grad_a[me] += stacked([sums[h][0] for h in range(HEADS)])
        grad_v[me] += stacked([sums[h][1] for h in range(HEADS)])
        return 0

    lax.fori_loop(first, count, pair, 0)


def part_way(msg1, self_a, self_g, stats, kept_scores, kept_terms, todo, count):
    def pair(n, _):
        entry = todo[n]
        me = lax.div(entry, 2)
        side = lax.div(me, 2)
        block = lax.rem(entry, 2)
        row_a = pl.multiple_of(side * (2 * ROWS) + block * BLOCK, BLOCK)
        row_v = pl.multiple_of(side * (2 * ROWS) + ROWS + block * BLOCK, BLOCK)
        mine = stats[me]
        scores = [dot(msg1[pl.ds(row_a, BLOCK), lanes(h)], self_a[me, h]) * LOG2E for h in range(HEADS)]
        changes = [dot(msg1[pl.ds(row_v, BLOCK), lanes(h)], self_g[me, h]) for h in range(HEADS)]
        for h in range(HEADS):
            g = HEADS + h
            kept_scores[n, h] = scores[h]
            kept_terms[n, h] = jnp.exp2(scores[h] - mine[h : h + 1]) * (changes[h] - mine[g : g + 1])
        return 0

    lax.fori_loop(0, count, pair, 0)


def back_rest(msg2, a_t, g_t, columns, self_v, kept_scores, kept_terms, grad_a, grad_v, todo, count):
    def pair(n, _):
        entry = todo[n]
        me = lax.div(entry, 2)
        side = lax.div(me, 2)
        block = lax.rem(entry, 2)
        row_g = pl.multiple_of(side * ROWS + block * BLOCK, BLOCK)
        at = side * 2 + block
        theirs = columns[at]
        made, ready, sums = {}, {}, {}

        def dots(h):
            made[h] = dot(msg2[pl.ds(row_g, BLOCK), lanes(h)], self_v[me, h])

        def weigh(h):
            g = HEADS + h
            other_p = jnp.exp2(kept_scores[n, h] - theirs[:, h : h + 1])
            slope = kept_terms[n, h] + other_p * (made[h] - theirs[:, g : g + 1])
            ready[h] = slope.astype(BF16), other_p.astype(BF16)

        def outs(h):
            slope, other_p = ready[h]
            sums[h] = dot(a_t[at, feats(h), :], slope), dot(g_t[at, feats(h), :], other_p)

        in_order(dots, weigh, outs)
        grad_a[me] += stacked([sums[h][0] for h in range(HEADS)])
        grad_v[me] += stacked([sums[h][1] for h in range(HEADS)])
        return 0

    lax.fori_loop(0, count, pair, 0)


def back_own(msg1, msg2, columns, self_a, self_v, self_g, grad_t, stats, held, grad_a, grad_v, todo, count):
    def pair(n, _):
        entry = todo[n]
        me = lax.div(entry, 2)
        block = lax.rem(entry, 2)
        frame = 2 + block
        row_v = pl.multiple_of(FVALS + block * BLOCK, BLOCK)
        row_g = pl.multiple_of(block * BLOCK, BLOCK)
        mine, theirs = stats[me], columns[block]
        made, ready, sums = {}, {}, {}

        def dots(h):
            made[h] = (
                held[n, h],
                dot(msg1[pl.ds(row_v, BLOCK), lanes(h)], self_g[me, h]),
                dot(msg2[pl.ds(row_g, BLOCK), lanes(h)], self_v[me, h]),
            )

        def weigh(h):
            ready[h] = slopes(made[h], mine, theirs, h)

        def outs(h):
            slope, self_p, other_p = ready[h]
            half = slice((h % 2) * DH, (h % 2 + 1) * DH)
            sums[h] = (
                dot(self_a[frame, h, half, :], slope),
                dot(grad_t[frame, feats(h), :], other_p),
                dot_other_way(self_a[me, h, half, :], slope),
                dot_other_way(grad_t[me, feats(h), :], self_p),
            )

        in_order(dots, weigh, outs)
        grad_a[me] += stacked([sums[h][0] for h in range(HEADS)])
        grad_v[me] += stacked([sums[h][1] for h in range(HEADS)])
        grad_a[frame] += stacked([sums[h][2] for h in range(HEADS)])
        grad_v[frame] += stacked([sums[h][3] for h in range(HEADS)])
        return 0

    lax.fori_loop(0, count, pair, 0)


def own_backward(
    plan, own1, own2, self_a, self_v, grad_t, stats, own_scores, self_g, grad_a, grad_v, columns, todo
):
    for me in range(4):
        for h in range(HEADS):
            self_g[me, h] = masked(grad_t[me], h)
        grad_a[me] = jnp.zeros((FEATS, BLOCK), F32)
        grad_v[me] = jnp.zeros((FEATS, BLOCK), F32)
    for block in range(2):
        columns[block] = as_columns(stats[2 + block])
    count = pair_list(todo, plan[0], jnp.int32(0))
    back_own(own1, own2, columns, self_a, self_v, self_g, grad_t, stats, own_scores, grad_a, grad_v, todo, count)


def touched_blocks(as_events, as_frames):
    return [jnp.bitwise_and(as_events, 3 * 4**a) != 0 for a in range(2)] + [
        jnp.bitwise_and(as_frames, 5 * 2**f) != 0 for f in range(2)
    ]


def wait_grads(me, ready, outs, sems):
    side, low = me // 2, (me % 2) * BLOCK
    for k in range(2):
        at = 2 * me + k
        pltpu.make_async_copy(ready.at[at], outs[2 * side + k].at[low : low + BLOCK], sems.at[at]).wait()


def send_grads(me, grad_a, grad_v, ready, outs, sems):
    side, low = me // 2, (me % 2) * BLOCK
    for k, grad in enumerate((grad_a, grad_v)):
        ready[2 * me + k] = grad[me].astype(BF16).T
        start_all((ready.at[2 * me + k], outs[2 * side + k].at[low : low + BLOCK], sems.at[2 * me + k]))


def near_backward(
    plan,
    near1,
    far1,
    near2,
    self_a,
    self_v,
    self_g,
    near_a_t,
    normed_t,
    stats,
    near_scores,
    grad_a_in,
    grad_v_in,
    grad_a,
    grad_v,
    event_out,
    frame_out,
    grad_queries,
    grad_event_values,
    grad_keys,
    grad_frame_values,
    far_a_t,
    kept_scores,
    kept_terms,
    g_t,
    columns,
    ready,
    todo,
    sems,
):
    grad_a[...] = grad_a_in[...]
    grad_v[...] = grad_v_in[...]
    other_grads(near2, g_t, columns)
    count = pair_list(todo, plan[1], read_code(near1, 0))
    known = near1, near2, near_a_t, g_t, columns, self_a, self_v, self_g, stats, grad_a, grad_v, todo
    back(*known, 0, jnp.minimum(count, HELD), near_scores)
    back(*known, HELD, count)
    outs = (grad_queries, grad_event_values, grad_keys, grad_frame_values)
    code = read_code(far1, 1)
    later = touched_blocks(plan[2], code)
    copies = []
    for me in range(4):

        @pl.when(jnp.logical_not(later[me]))
        def _():
            send_grads(me, grad_a, grad_v, ready, outs, sems)

    for me in range(4):
        low = (me % 2) * BLOCK
        ready[8 + me] = normed_t[me].T
        copies += start_all(
            (ready.at[8 + me], (event_out, frame_out)[me // 2].at[low : low + BLOCK], sems.at[8 + me])
        )
    other_queries(far1, far_a_t)
    count = pair_list(todo, plan[2], code)
    part_way(far1, self_a, self_g, stats, kept_scores, kept_terms, todo, jnp.minimum(count, KEPT))
    for c in copies:
        c.wait()
    for me in range(4):

        @pl.when(jnp.logical_not(later[me]))
        def _():
            wait_grads(me, ready, outs, sems)


def far_backward(
    plan,
    far1,
    far2,
    self_a,
    self_v,
    self_g,
    far_a_t,
    stats,
    kept_scores,
    kept_terms,
    grad_a_in,
    grad_v_in,
    _queries,
    _event_values,
    _keys,
    _frame_values,
    grad_queries,
    grad_event_values,
    grad_keys,
    grad_frame_values,
    grad_a,
    grad_v,
    g_t,
    columns,
    ready,
    todo,
    sems,
):
    code = read_code(far1, 1)
    touched = touched_blocks(plan[2], code)
    outs = (grad_queries, grad_event_values, grad_keys, grad_frame_values)
    count = pair_list(todo, plan[2], code)

    @pl.when(count > 0)
    def _():
        for me in range(4):

            @pl.when(touched[me])
            def _():
                grad_a[me] = grad_a_in[me]
                grad_v[me] = grad_v_in[me]

        other_grads(far2, g_t, columns)
        begun = jnp.minimum(count, KEPT)
        back_rest(far2, far_a_t, g_t, columns, self_v, kept_scores, kept_terms, grad_a, grad_v, todo, begun)
        back(
            far1, far2, far_a_t, g_t, columns, self_a, self_v, self_g, stats, grad_a, grad_v, todo, begun, count
        )
        for me in range(4):

            @pl.when(touched[me])
            def _():
                send_grads(me, grad_a, grad_v, ready, outs, sems)

        for me in range(4):

            @pl.when(touched[me])
            def _():
                wait_grads(me, ready, outs, sems)


def shape(*dims, dtype=F32):
    return jax.ShapeDtypeStruct(dims, dtype)


def specs(kinds):
    space = {"s": pltpu.SMEM, "v": pltpu.VMEM, "h": pltpu.HBM}
    return [pl.BlockSpec(memory_space=space[k]) for k in kinds]


def kernel(body, operands, places, outs, out_places, scratch=(), flops=0, limit=VMEM_LIMIT, aliases=()):
    return pl.pallas_call(
        body,
        out_shape=tuple(outs),
        in_specs=specs(places),
        out_specs=tuple(specs(out_places)),
        scratch_shapes=list(scratch),
        compiler_params=params(limit),
        cost_estimate=cost(flops),
        input_output_aliases=dict(aliases),
    )(*operands)


def on_device(
    event_queries,
    event_values,
    frame_keys,
    frame_values,
    partner,
    live_count,
    event_cotangent,
    frame_cotangent,
):
    width = FEATS * lax.axis_size("hd")
    runs = lax.axis_size("st")
    inner_pairs = [(i, i ^ 1) for i in range(runs)]
    outer_pairs = [(i, i + 1) for i in range(1, runs - 1, 2)] + [(i + 1, i) for i in range(1, runs - 1, 2)]
    tile = (4, FEATS, BLOCK)
    wide = (4, HEADS, PAIR, BLOCK)
    small = (4, 2 * HEADS, BLOCK)
    todo = pltpu.SMEM((16,), jnp.int32)

    far_msg1, plan = kernel(
        pack_kernel,
        (partner, live_count, event_queries, event_values, frame_keys, frame_values),
        "hhhhhh",
        (shape(FAR1, FEATS, dtype=BF16), shape(8, dtype=jnp.int32)),
        "vs",
        [
            pltpu.SMEM((2, SLOTS), jnp.int32),
            pltpu.SMEM((2,), jnp.int32),
            pltpu.SemaphoreType.DMA((6,)),
        ],
        limit=PACK_LIMIT,
    )
    far1 = lax.ppermute(far_msg1, "st", outer_pairs)
    msg1 = far_msg1[0:MSG1]
    near1 = lax.ppermute(msg1, "st", inner_pairs)

    held = shape(HELD + 1, HEADS, BLOCK, BLOCK)
    self_a, self_v, cot_t, soft, acc, near_a_t, own_scores, near_scores = kernel(
        near_forward,
        (plan, msg1, near1, event_cotangent, frame_cotangent),
        "svvhh",
        (
            shape(*wide, dtype=BF16),
            shape(*wide, dtype=BF16),
            shape(*tile, dtype=BF16),
            shape(*small),
            shape(*tile),
            shape(*tile, dtype=BF16),
            held,
            held,
        ),
        "vvvvvvvv",
        [
            pltpu.VMEM((2, ROWS, FEATS), BF16),
            pltpu.VMEM(tile, BF16),
            pltpu.VMEM(tile, BF16),
            todo,
            pltpu.SemaphoreType.DMA((2,)),
        ],
        1e6,
    )
    att, lse, sums = kernel(
        far_forward,
        (plan, far1, self_a, cot_t, soft, acc),
        "svvvvv",
        (shape(*tile), shape(*small), shape(lax.axis_size("hd"), 8, BLOCK)),
        "vvv",
        [
            pltpu.VMEM(small, F32),
            pltpu.VMEM(tile, BF16),
            pltpu.VMEM((1, HEADS, BLOCK, BLOCK), F32),
            todo,
        ],
        1e6,
    )
    sums = lax.all_to_all(sums, "hd", 0, 0)

    grad_t, normed_t, stats, msg2, far_msg2 = kernel(
        lambda *refs: grad_kernel(width, *refs),
        (att, cot_t, lse, sums),
        "vvvv",
        (
            shape(*tile, dtype=BF16),
            shape(*tile, dtype=BF16),
            shape(*small),
            shape(MSG2, FEATS, dtype=BF16),
            shape(FAR2, FEATS, dtype=BF16),
        ),
        "vvvvv",
        flops=1e6,
    )
    far2 = lax.ppermute(far_msg2, "st", outer_pairs)
    near2 = lax.ppermute(msg2, "st", inner_pairs)

    self_g, grad_a, grad_v = kernel(
        own_backward,
        (plan, msg1, msg2, self_a, self_v, grad_t, stats, own_scores),
        "svvvvvvv",
        (shape(*wide, dtype=BF16), shape(*tile), shape(*tile)),
        "vvv",
        [pltpu.VMEM((2, BLOCK, PAIR), F32), todo],
        1e6,
    )
    whole = [shape(ROWS, FEATS, dtype=BF16)]
    grad_a, grad_v, event_out, frame_out, *grads, far_a_t, kept_scores, kept_terms = kernel(
        near_backward,
        (plan, near1, far1, near2, self_a, self_v, self_g, near_a_t, normed_t, stats, near_scores, grad_a, grad_v),
        "svvvvvvvvvvvv",
        [shape(*tile)] * 2 + whole * 6 + [shape(*tile, dtype=BF16)] + [shape(KEPT, HEADS, BLOCK, BLOCK)] * 2,
        "vvhhhhhhvvv",
        [
            pltpu.VMEM(tile, BF16),
            pltpu.VMEM((4, BLOCK, PAIR), F32),
            pltpu.VMEM((12, BLOCK, FEATS), BF16),
            todo,
            pltpu.SemaphoreType.DMA((12,)),
        ],
        1e6,
    )
    grads = kernel(
        far_backward,
        (plan, far1, far2, self_a, self_v, self_g, far_a_t, stats, kept_scores, kept_terms, grad_a, grad_v, *grads),
        "svvvvvvvvvvvhhhh",
        whole * 4,
        "hhhh",
        [
            pltpu.VMEM(tile, F32),
            pltpu.VMEM(tile, F32),
            pltpu.VMEM(tile, BF16),
            pltpu.VMEM((4, BLOCK, PAIR), F32),
            pltpu.VMEM((8, BLOCK, FEATS), BF16),
            todo,
            pltpu.SemaphoreType.DMA((8,)),
        ],
        1e6,
        aliases=((12, 0), (13, 1), (14, 2), (15, 3)),
    )
    return (event_out, frame_out) + tuple(grads)


def solution(mesh):
    tokens = P("st", "hd")
    return jax.shard_map(
        on_device,
        mesh=mesh,
        in_specs=(tokens, tokens, tokens, tokens, P("st", None), P("st"), tokens, tokens),
        out_specs=(tokens,) * 6,
        check_vma=False,
    )
```
